256 devices in a mesh: example: 32 (over y, z_hi, core), layer: 8 (over z_lo, x).
Axes of the slice: x: 4, y: 4, z: 8 (z_hi: 4, z_lo: 2; z = z_hi * 2 + z_lo), core: 2. Of those that a mesh axis runs over, the one named last changes fastest.
Arguments:
- query_grads: bfloat16 [8, 1024, 4096], P('layer', 'example'), may hold values from -6 to 6
- doc_grads: bfloat16 [8, 16384, 4096], P('layer', 'example'), may hold values from -0.14941406 to 0.14941406
- out_basis: float32 [8, 32, 32], P('layer', 'example'), may hold values from -1 to 1
- in_basis: float32 [8, 128, 128], P('layer', 'example'), may hold values from -0.5 to 0.5
- eigenvalues: float32 [8, 32, 128], P('layer', 'example'), may hold values from 0.5 to 16
- damping: float32 [8], P('layer'), may hold values from 0.1 to 1
Outputs:
- scores: float32 [1024, 16384], P('layer', 'example')
The draws below stay inside these ranges and needn't reach their ends.
All inputs are finite; a program needn't handle non-finite values.
Results may differ from the reference program's by a relative error of at most 0.0029.
Values may be sent and summed in bfloat16 or wider, within the bound.
No kernel may reach another device: no remote copies, remote signals or barrier semaphores. Data moves between devices by JAX's collectives and lax.ppermute only.
A program may use at most 128 MiB of HBM per device.

```python
import math
import jax
import jax.numpy as jnp
from jax import lax

PROJ_OUT = 32
PROJ_IN = 128
PROJ = 4096
LAYERS = 8
QUERIES = 1024
DOCS = 16384


def levels(key, dims, split, low, high):
    def one(position, shards_of):
        draws = jax.random.uniform(jax.random.fold_in(jax.random.fold_in(key, 6), position), (shards_of,), jnp.float32, low / len(split), high / len(split))
        return jnp.repeat(jnp.exp(draws), dims[position] // shards_of).reshape((-1,) + (1,) * (len(dims) - position - 1))

    factor_of = one(*split[0])
    for cut in split[1:]:
        factor_of = factor_of * one(*cut)
    return factor_of


def scatter_about(stream_key, dims, deviation, limit, split=(), dtype=jnp.bfloat16):
    values = deviation * jax.random.normal(stream_key, dims, jnp.float32)
    if split:
        values = values * levels(stream_key, dims, split, -0.22, 0.18)
    return jnp.clip(values, -limit, limit).astype(dtype)


def setup_inputs(seed: int = 0) -> dict:
    seeds = jax.random.split(jax.random.key(seed), 7)
    return {
        "query_grads": scatter_about(seeds[0], (LAYERS, QUERIES, PROJ), 1.0, 6.0, ((0, 8), (1, 32))),
        "doc_grads": scatter_about(seeds[1], (LAYERS, DOCS, PROJ), 0.025, 0.14941406, ((0, 8), (1, 32))),
        "out_basis": scatter_about(seeds[2], (LAYERS, PROJ_OUT, PROJ_OUT), PROJ_OUT ** -0.5, 1.0, ((0, 8), (1, 32)), jnp.float32),
        "in_basis": scatter_about(seeds[3], (LAYERS, PROJ_IN, PROJ_IN), PROJ_IN ** -0.5, 0.5, ((0, 8), (1, 32)), jnp.float32),
        "eigenvalues": jnp.clip(jnp.exp(math.log(16.0) - 3.465736 * jax.random.uniform(seeds[4], (LAYERS, PROJ_OUT, PROJ_IN), jnp.float32) ** levels(seeds[4], (LAYERS, PROJ_OUT, PROJ_IN), ((0, 8), (1, 32)), -0.2, 0.2)), 0.5, 16.0),
        "damping": jnp.clip(jnp.exp(math.log(1.0) - 2.3025851 * jax.random.uniform(seeds[5], (LAYERS,), jnp.float32) ** levels(seeds[5], (LAYERS,), ((0, 8),), -0.2, 0.2)), 0.1, 1.0),
    }


precise = lax.Precision.HIGHEST


def precondition(raw_rows, out_basis, in_basis, denominator):
    number = raw_rows.shape[0]
    matrix_form = raw_rows.astype(jnp.float32).reshape(number, out_basis.shape[0], in_basis.shape[0])
    half_rotated = jnp.einsum("nij,jb->nib", matrix_form, in_basis, precision=precise)
    rotated = jnp.einsum("nib,ia->nab", half_rotated, out_basis, precision=precise)
    scaled = rotated / denominator
    restored = jnp.einsum("nab,jb->naj", scaled, in_basis, precision=precise)
    result = jnp.einsum("naj,ia->nij", restored, out_basis, precision=precise)
    return result.reshape(number, raw_rows.shape[1]).astype(jnp.bfloat16)


def layer_scores(conditioned, documents):
    return lax.dot_general(conditioned, documents, (((1,), (1,)), ((), ())), preferred_element_type=jnp.float32)


def reference(query_grads, doc_grads, out_basis, in_basis, eigenvalues, damping):
    running = jnp.zeros((query_grads.shape[1], doc_grads.shape[1]), jnp.float32)
    for layer_pos in range(query_grads.shape[0]):
        denominator = eigenvalues[layer_pos] + damping[layer_pos]
        conditioned = precondition(query_grads[layer_pos], out_basis[layer_pos], in_basis[layer_pos], denominator)
        running = running + layer_scores(conditioned, doc_grads[layer_pos])
    return running
```

```python
import functools
import jax
import jax.numpy as jnp
from jax import lax
from jax.experimental import pallas as pl
from jax.experimental.pallas import tpu as pltpu
from jax.sharding import PartitionSpec as P

NY, NZ, NC = 4, 4, 2
NL, NX = 2, 4
ROWS = 32
OUT, IN = 32, 128
F32, BF16 = jnp.float32, jnp.bfloat16
VMEM = pl.BlockSpec(memory_space=pltpu.VMEM)
SMEM = pl.BlockSpec(memory_space=pltpu.SMEM)


def example_shift(dy, dz, dc):
    def place(y, z, c):
        return (y % NY) * NZ * NC + (z % NZ) * NC + c % NC

    return [
        (place(y, z, c), place(y + dy, z + dz, c + dc))
        for y in range(NY)
        for z in range(NZ)
        for c in range(NC)
    ]


def layer_shift(dl, dx):
    return [
        (a * NX + x, ((a + dl) % NL) * NX + (x + dx) % NX) for a in range(NL) for x in range(NX)
    ]


def send(x, dy=0, dz=0, dc=0):
    return lax.ppermute(x, "example", example_shift(dy, dz, dc))


def split2(x):
    high = x.astype(BF16)
    return high, (x - high.astype(F32)).astype(BF16)


def mm(a, b, contract=((1,), (0,))):
    return lax.dot_general(a, b, (contract, ((), ())), preferred_element_type=F32)


def coordinates(example):
    return example >> 3, (example >> 1) & 3, example & 1


def prepare_kernel(place_ref, damp_ref, *refs):
    pieces, (left_ref, right_ref, in_ref, scale_ref), rows = refs[:NZ], refs[NZ:-1], refs[-1]
    y, z, c = coordinates(place_ref[0])
    for dz in range(NZ):
        for dy in range(NY):
            for dc in range(NC):
                owner = ((y - dy) & 3) * 8 + ((z - dz) & 3) * 2 + (c ^ dc)
                k = dy * NC + dc
                piece = pieces[dz][8 * k : 8 * k + 8, :]
                rows[pl.ds(pl.multiple_of(owner * 8, 8), 8), :] = piece
    table = rows[...]
    high, low = split2(table)
    lowest = (table - high.astype(F32) - low.astype(F32)).astype(BF16)

    def iota(shape, axis):
        return lax.broadcasted_iota(jnp.int32, shape, axis)

    def pick(condition):
        return condition.astype(F32).astype(BF16)

    r, k = iota((IN, 256), 0), iota((IN, 256), 1)
    pick_in = pick(k == (r // 4) * 8 + r % 4)
    in_ref[0] = mm(pick_in, high).astype(BF16)
    in_ref[1] = mm(pick_in, low).astype(BF16)
    r, k = iota((256, 256), 0), iota((256, 256), 1)
    pick_eig = pick(k == (r // 8) * 8 + 4)
    eig = mm(pick_eig, high) + (mm(pick_eig, low) + mm(pick_eig, lowest))
    scale_ref[...] = 1.0 / (eig + damp_ref[0])
    pick_out = pick(k == (r // 8) * 8 + 5)
    spread = pick(iota((IN, 256), 0) == iota((IN, 256), 1) // 8)
    same = (r % 8 == k % 8).astype(F32)
    for term, part in enumerate((high, low)):
        whole = mm(mm(pick_out, part).astype(BF16), spread) * same
        right_ref[term] = whole.astype(BF16)
        left_ref[term] = whole.T.astype(BF16)


def prepare(place, damping, pieces):
    shape = jax.ShapeDtypeStruct
    return pl.pallas_call(
        prepare_kernel,
        out_shape=(
            shape((2, 256, 256), BF16),
            shape((2, 256, 256), BF16),
            shape((2, IN, IN), BF16),
            shape((256, IN), F32),
        ),
        in_specs=[SMEM, SMEM] + [VMEM] * NZ,
        out_specs=(VMEM,) * 4,
        scratch_shapes=[pltpu.VMEM((256, 128), F32)],
        compiler_params=pltpu.CompilerParams(vmem_limit_bytes=16 << 20),
        cost_estimate=pl.CostEstimate(flops=200_000_000, bytes_accessed=1 << 20, transcendentals=0),
        name="prepare",
    )(place, damping, *pieces)


def three(a, b, contract=((1,), (0,))):
    ah, al = a
    bh, bl = b
    return mm(ah, bh, contract) + (mm(al, bh, contract) + mm(ah, bl, contract))


def rotate_sixteen(x, left, right, basis, scale):
    tall = jnp.concatenate([x[:, IN * i : IN * (i + 1)] for i in range(OUT)], axis=0)
    half = mm(tall, basis[0]) + mm(tall, basis[1])
    half = half.reshape(OUT, 2, 8, IN)
    side = jnp.concatenate([half[:, h].reshape(OUT * 8, IN) for h in range(2)], axis=1)
    rotated = three(left, split2(side))
    scaled = jnp.concatenate(
        [rotated[:, IN * h : IN * (h + 1)] * scale for h in range(2)], axis=0
    )
    restored = three(split2(scaled), basis, ((1,), (1,)))
    side = jnp.concatenate([restored[256 * h : 256 * (h + 1)] for h in range(2)], axis=1)
    return three(right, split2(side)).astype(F32)


def rotate_kernel(left_ref, right_ref, in_ref, scale_ref, *refs):
    blocks, out_ref = refs[:-1], refs[-1]
    left, right = (left_ref[0], left_ref[1]), (right_ref[0], right_ref[1])
    basis, scale = (in_ref[0], in_ref[1]), scale_ref[...]
    start = 0
    for block in blocks:

        @pl.loop(0, block.shape[0] // 16)
        def _(step, block=block, start=start):
            at = pl.multiple_of(step * 16, 16)
            done = rotate_sixteen(block[pl.ds(at, 16), :], left, right, basis, scale)
            to = pl.multiple_of(start + at, 16)
            for i in range(OUT):
                rows = jnp.concatenate(
                    [done[8 * i : 8 * i + 8, :IN], done[8 * i : 8 * i + 8, IN:]], axis=0
                )
                out_ref[pl.ds(to, 16), IN * i : IN * (i + 1)] = rows.astype(BF16)

        start += block.shape[0]


def rotate(tables, blocks):
    rows = sum(b.shape[0] for b in blocks)
    width = blocks[0].shape[1]
    return pl.pallas_call(
        rotate_kernel,
        out_shape=jax.ShapeDtypeStruct((rows, width), BF16),
        in_specs=[VMEM] * (4 + len(blocks)),
        out_specs=VMEM,
        compiler_params=pltpu.CompilerParams(vmem_limit_bytes=32 << 20),
        cost_estimate=pl.CostEstimate(
            flops=rows * 30_000_000, bytes_accessed=4 * rows * width, transcendentals=0
        ),
        name="rotate",
    )(*tables, *blocks)


def scores_of(conditioned, documents):
    return lax.dot_general(
        conditioned, documents, (((1,), (1,)), ((), ())), preferred_element_type=F32
    ).astype(BF16)


def arrange_kernel(offsets, place_ref, *refs):
    parts, out_ref = refs[:-1], refs[-1]
    y, z, c = coordinates(place_ref[0])
    layer = place_ref[1]
    for k, part in enumerate(parts):
        kind = c ^ (k % 2)
        for at, (dy, dz) in enumerate(offsets[k // 2]):
            from_z = (z - dz) & 3
            to = ((y - dy) & 3) * 2 + (from_z >> 1)
            turn = ((to ^ layer) & 4) + ((to - layer) & 3)
            out_ref[turn * 4 + (from_z & 1) * 2 + kind] = part[ROWS * at : ROWS * (at + 1), :]


def arrange(place, offsets, parts):
    count = sum(p.shape[0] for p in parts) // ROWS
    columns = parts[0].shape[1]
    return pl.pallas_call(
        functools.partial(arrange_kernel, offsets),
        out_shape=jax.ShapeDtypeStruct((count, ROWS, columns), BF16),
        in_specs=[SMEM] + [VMEM] * len(parts),
        out_specs=VMEM,
        compiler_params=pltpu.CompilerParams(vmem_limit_bytes=16 << 20),
        cost_estimate=pl.CostEstimate(
            flops=0, bytes_accessed=count * ROWS * columns * 4, transcendentals=0
        ),
        name="arrange",
    )(place, *parts)


def around(own, axis):
    behind, ahead = send(own, **{axis: 1}), send(own, **{axis: -1})
    cut = own.shape[0] // 2
    far = (send(behind[:cut], **{axis: 1}), send(ahead[cut:], **{axis: -1}))
    return behind, ahead, far


def body(query_grads, doc_grads, out_basis, in_basis, eigenvalues, damping):
    place = jnp.stack([lax.axis_index("example"), lax.axis_index("layer")])

    row = jnp.concatenate(
        [
            in_basis[0],
            eigenvalues[0],
            jnp.pad(out_basis[0], ((0, 0), (0, IN - OUT))),
            jnp.zeros((2, IN), F32),
        ],
        axis=0,
    )
    pair = jnp.concatenate([row, send(row, dc=1)], axis=0)
    plane = jnp.concatenate([pair] + [send(pair, dy=d) for d in range(1, NY)], axis=0)
    pieces = [plane] + [send(plane, dz=d) for d in range(1, NZ)]
    tables = prepare(place, damping, pieces)

    docs = doc_grads[0]
    docs_other = send(docs, dc=1)

    own = query_grads[0]
    near = around(own, "dz")
    by_y = around(own, "dy")
    side = jnp.concatenate(near[:2], axis=0)
    side_y = around(side, "dy")
    far = jnp.concatenate(near[2], axis=0)
    far_y = around(far, "dy")

    steps = (0, 1, -1, 2)
    groups = (
        ((own, *by_y[:2], *by_y[2]), [(dy, 0) for dy in steps]),
        ((side, *side_y[:2], *side_y[2]), [(dy, dz) for dy in steps for dz in (1, -1)]),
        ((far, *far_y[:2], *far_y[2]), [(dy, 2) for dy in steps]),
    )
    parts = []
    for blocks, _ in groups:
        conditioned = rotate(tables, blocks)
        parts.append(scores_of(conditioned, docs))
        parts.append(send(scores_of(conditioned, docs_other), dc=1))
    ready = arrange(place, [offsets for _, offsets in groups], parts)
    columns = docs.shape[0]
    ready = ready.reshape(NL * NX, 4 * ROWS, columns)
    total = ready[0].astype(F32)
    for dl in range(NL):
        for dx in range(NX):
            if dl or dx:
                total += lax.ppermute(ready[dl * NX + dx], "layer", layer_shift(dl, dx)).astype(F32)
    return total


def solution(mesh):
    placed = P("layer", "example", None)
    return jax.shard_map(
        body,
        mesh=mesh,
        in_specs=(placed,) * 5 + (P("layer"),),
        out_specs=P("layer", "example"),
        check_vma=False,
    )
```

```python
import functools
import jax
import jax.numpy as jnp
from jax import lax
from jax.experimental import pallas as pl
from jax.experimental.pallas import tpu as pltpu
from jax.sharding import PartitionSpec as P

NY, NZ, NC = 4, 4, 2
NL, NX = 2, 4
ROWS = 32
CHUNK = 64
OUT, IN = 32, 128
F32, BF16 = jnp.float32, jnp.bfloat16
VMEM = pl.BlockSpec(memory_space=pltpu.VMEM)
SMEM = pl.BlockSpec(memory_space=pltpu.SMEM)
ANY = pl.BlockSpec(memory_space=pl.ANY)


def example_shift(dy, dz, dc):
    def place(y, z, c):
        return (y % NY) * NZ * NC + (z % NZ) * NC + c % NC

    return [
        (place(y, z, c), place(y + dy, z + dz, c + dc))
        for y in range(NY)
        for z in range(NZ)
        for c in range(NC)
    ]


def layer_shift(dl, dx):
    return [
        (a * NX + x, ((a + dl) % NL) * NX + (x + dx) % NX) for a in range(NL) for x in range(NX)
    ]


def send(x, dy=0, dz=0, dc=0):
    return lax.ppermute(x, "example", example_shift(dy, dz, dc))


def split2(x):
    high = x.astype(BF16)
    return high, (x - high.astype(F32)).astype(BF16)


def mm(a, b, contract=((1,), (0,))):
    return lax.dot_general(a, b, (contract, ((), ())), preferred_element_type=F32)


def coordinates(example):
    return example >> 3, (example >> 1) & 3, example & 1


def held_kernel(x_ref, *refs):
    pltpu.sync_copy(x_ref, refs[-1])


def held(x, after=()):
    return pl.pallas_call(
        held_kernel,
        out_shape=jax.ShapeDtypeStruct(x.shape, x.dtype),
        in_specs=[ANY] * (1 + len(after)),
        out_specs=VMEM,
        compiler_params=pltpu.CompilerParams(vmem_limit_bytes=16 << 20),
        cost_estimate=pl.CostEstimate(flops=0, bytes_accessed=2 * x.nbytes, transcendentals=0),
        name="held",
    )(x, *after)


def pack_kernel(in_ref, eig_ref, basis_ref, out_ref):
    out_ref[...] = jnp.zeros_like(out_ref)
    out_ref[0:4, :] = in_ref[...]
    out_ref[4:5, :] = eig_ref[...]
    out_ref[5:6, 0:OUT] = basis_ref[...]


def pack(*parts):
    return pl.pallas_call(
        pack_kernel,
        out_shape=jax.ShapeDtypeStruct((8, IN), F32),
        in_specs=[VMEM] * 3,
        out_specs=VMEM,
        compiler_params=pltpu.CompilerParams(vmem_limit_bytes=1 << 20),
        name="pack",
    )(*parts)


def join_kernel(count, *refs):
    parts, out_ref = refs[:count], refs[-1]
    rows = parts[0].shape[0]
    for k, part in enumerate(parts):
        out_ref[rows * k : rows * (k + 1), :] = part[...]


def join(parts, after):
    rows, columns = parts[0].shape
    return pl.pallas_call(
        functools.partial(join_kernel, len(parts)),
        out_shape=jax.ShapeDtypeStruct((rows * len(parts), columns), parts[0].dtype),
        in_specs=[VMEM] * len(parts) + [ANY] * len(after),
        out_specs=VMEM,
        compiler_params=pltpu.CompilerParams(vmem_limit_bytes=4 << 20),
        name="join",
    )(*parts, *after)


def prepare_kernel(place_ref, damp_ref, *refs):
    pieces, rows = refs[:NZ], refs[-1]
    left_ref, right_ref, in_ref, back_ref, scale_ref = refs[-6:-1]
    y, z, c = coordinates(place_ref[0])
    for dz in range(NZ):
        for dy in range(NY):
            for dc in range(NC):
                owner = ((y - dy) & 3) * 8 + ((z - dz) & 3) * 2 + (c ^ dc)
                k = dy * NC + dc
                piece = pieces[dz][8 * k : 8 * k + 8, :]
                rows[pl.ds(pl.multiple_of(owner * 8, 8), 8), :] = piece
    table = rows[...]
    high, low = split2(table)
    lowest = (table - high.astype(F32) - low.astype(F32)).astype(BF16)

    def iota(shape, axis):
        return lax.broadcasted_iota(jnp.int32, shape, axis)

    def pick(condition):
        return condition.astype(F32).astype(BF16)

    r, k = iota((IN, 256), 0), iota((IN, 256), 1)
    pick_in = pick(k == (r // 4) * 8 + r % 4)
    basis, rest = mm(pick_in, high), mm(pick_in, low)
    in_ref[...] = jnp.concatenate([basis, rest], axis=0).astype(BF16)
    turned, turned_rest = basis.T, rest.T
    back_ref[...] = jnp.concatenate(
        [
            jnp.concatenate([turned, turned_rest], axis=1),
            jnp.concatenate([turned, jnp.zeros_like(turned)], axis=1),
        ],
        axis=0,
    ).astype(BF16)
    r, k = iota((256, 256), 0), iota((256, 256), 1)
    pick_eig = pick(k == (r // 8) * 8 + 4)
    eig = mm(pick_eig, high) + (mm(pick_eig, low) + mm(pick_eig, lowest))
    scale_ref[...] = 1.0 / (eig + damp_ref[0])
    pick_out = pick(k == (r // 8) * 8 + 5)
    spread = pick(iota((IN, 256), 0) == iota((IN, 256), 1) // 8)
    same = (r % 8 == k % 8).astype(F32)
    for term, part in enumerate((high, low)):
        whole = mm(mm(pick_out, part).astype(BF16), spread) * same
        right_ref[256 * term : 256 * (term + 1), :] = whole.astype(BF16)
        left_ref[256 * term : 256 * (term + 1), :] = whole.T.astype(BF16)


def prepare(place, damping, pieces, after):
    shape = jax.ShapeDtypeStruct
    return pl.pallas_call(
        prepare_kernel,
        out_shape=(
            shape((512, 256), BF16),
            shape((512, 256), BF16),
            shape((2 * IN, IN), BF16),
            shape((2 * IN, 2 * IN), BF16),
            shape((256, IN), F32),
        ),
        in_specs=[SMEM, SMEM] + [VMEM] * NZ + [ANY] * len(after),
        out_specs=(VMEM,) * 5,
        scratch_shapes=[pltpu.VMEM((256, 128), F32)],
        compiler_params=pltpu.CompilerParams(vmem_limit_bytes=16 << 20),
        cost_estimate=pl.CostEstimate(flops=200_000_000, bytes_accessed=1 << 20, transcendentals=0),
        name="prepare",
    )(place, damping, *pieces, *after)


def mix(matrix, x):
    high, low = split2(x)
    both = mm(matrix, high)
    return both[:256] + (both[256:] + mm(matrix[:256], low))


def rotate_chunk(x, left, right, basis, back, scale):
    count = 2 * len(x)
    tall = jnp.concatenate(
        [piece[:, IN * i : IN * (i + 1)] for piece in x for i in range(OUT)], axis=0
    )
    half = mm(jnp.concatenate([tall, tall], axis=1), basis)
    half = half.reshape(count // 2, OUT, 2, 8, IN)
    side = jnp.concatenate(
        [half[g // 2, :, g % 2].reshape(OUT * 8, IN) for g in range(count)], axis=1
    )
    rotated = mix(left, side)
    scaled = jnp.concatenate(
        [rotated[:, IN * g : IN * (g + 1)] * scale for g in range(count)], axis=0
    )
    restored = mm(jnp.concatenate(split2(scaled), axis=1), back)
    restored = restored[:, :IN] + restored[:, IN:]
    side = jnp.concatenate([restored[256 * g : 256 * (g + 1)] for g in range(count)], axis=1)
    return mix(right, side)


def rotate_kernel(most, count, left_ref, right_ref, in_ref, back_ref, scale_ref, *refs):
    blocks, out_ref = refs[:count], refs[-1]
    pieces = [(b, at) for b in blocks for at in range(0, b.shape[0], 16)]
    step = most // 16
    for first in range(0, len(pieces), step):
        chunk = pieces[first : first + step]
        done = rotate_chunk(
            [b[at : at + 16, :] for b, at in chunk],
            left_ref[...],
            right_ref[...],
            in_ref[...],
            back_ref[...],
            scale_ref[...],
        )
        for p in range(len(chunk)):
            to = 16 * (first + p)
            for i in range(OUT):
                rows = done[8 * i : 8 * i + 8, 2 * IN * p : 2 * IN * (p + 1)]
                rows = jnp.concatenate([rows[:, :IN], rows[:, IN:]], axis=0)
                out_ref[to : to + 16, IN * i : IN * (i + 1)] = rows.astype(BF16)


def rotate(tables, blocks, after):
    rows = sum(b.shape[0] for b in blocks)
    width = blocks[0].shape[1]
    return pl.pallas_call(
        functools.partial(rotate_kernel, CHUNK, len(blocks)),
        out_shape=jax.ShapeDtypeStruct((rows, width), BF16),
        in_specs=[VMEM] * (5 + len(blocks)) + [ANY] * len(after),
        out_specs=VMEM,
        compiler_params=pltpu.CompilerParams(vmem_limit_bytes=32 << 20),
        cost_estimate=pl.CostEstimate(
            flops=rows * 30_000_000, bytes_accessed=4 * rows * width, transcendentals=0
        ),
        name="rotate",
    )(*tables, *blocks, *after)


def scores_of(conditioned, documents):
    return lax.dot_general(
        conditioned, documents, (((1,), (1,)), ((), ())), preferred_element_type=F32
    ).astype(BF16)


def arrange_kernel(offsets, place_ref, *refs):
    parts, out_ref = refs[: 2 * len(offsets)], refs[-1]
    y, z, c = coordinates(place_ref[0])
    layer = place_ref[1]
    for k, part in enumerate(parts):
        kind = c ^ (k % 2)
        for at, (dy, dz) in enumerate(offsets[k // 2]):
            to = ((y - dy) & 3) * 2 + (((z - dz) & 3) >> 1)
            turn = ((to ^ layer) & 4) + ((to - layer) & 3)
            out_ref[turn * 2 + kind] = part[ROWS * at : ROWS * (at + 1), :]


def arrange(place, offsets, parts, after):
    count = sum(p.shape[0] for p in parts) // ROWS
    columns = parts[0].shape[1]
    return pl.pallas_call(
        functools.partial(arrange_kernel, offsets),
        out_shape=jax.ShapeDtypeStruct((count, ROWS, columns), BF16),
        in_specs=[SMEM] + [VMEM] * len(parts) + [ANY] * len(after),
        out_specs=VMEM,
        compiler_params=pltpu.CompilerParams(vmem_limit_bytes=16 << 20),
        cost_estimate=pl.CostEstimate(
            flops=0, bytes_accessed=count * ROWS * columns * 4, transcendentals=0
        ),
        name="arrange",
    )(place, *parts, *after)


def finish_kernel(place_ref, *refs):
    out_ref, waves = refs[-1], (refs[: NL * NX], refs[NL * NX : -1])
    z = coordinates(place_ref[0])[1]
    for odd, wave in enumerate(waves):
        total = wave[0][...].astype(F32)
        for part in wave[1:]:
            total += part[...].astype(F32)
        rows = total.shape[0]
        out_ref[pl.ds(pl.multiple_of(((z + odd) & 1) * rows, rows), rows), :] = total


def finish(place, even, odd):
    rows, columns = even[0].shape
    return pl.pallas_call(
        finish_kernel,
        out_shape=jax.ShapeDtypeStruct((2 * rows, columns), F32),
        in_specs=[SMEM] + [VMEM] * (len(even) + len(odd)),
        out_specs=VMEM,
        compiler_params=pltpu.CompilerParams(vmem_limit_bytes=8 << 20),
        name="finish",
    )(place, *even, *odd)


def spread_over_layers(ready):
    ready = ready.reshape(NL * NX, 2 * ROWS, ready.shape[-1])
    parts = [ready[0]]
    for dl in range(NL):
        for dx in range(NX):
            if dl or dx:
                parts.append(lax.ppermute(ready[dl * NX + dx], "layer", layer_shift(dl, dx)))
    return parts


def halves_kernel(behind_ref, ahead_ref, *refs):
    first_ref, second_ref = refs[-2:]
    rows = first_ref.shape[0]
    first_ref[...] = behind_ref[:rows, :]
    second_ref[...] = ahead_ref[rows:, :]


def halves(behind, ahead, after):
    rows, columns = behind.shape
    return pl.pallas_call(
        halves_kernel,
        out_shape=(jax.ShapeDtypeStruct((rows // 2, columns), behind.dtype),) * 2,
        in_specs=[VMEM, VMEM] + [ANY] * len(after),
        out_specs=(VMEM, VMEM),
        compiler_params=pltpu.CompilerParams(vmem_limit_bytes=4 << 20),
        name="halves",
    )(behind, ahead, *after)


def both_ways(own, axis):
    return send(own, **{axis: 1}), send(own, **{axis: -1})


def far_side(near, axis, after=()):
    first, second = halves(*near, after)
    return send(first, **{axis: 1}), send(second, **{axis: -1})


def body(query_grads, doc_grads, out_basis, in_basis, eigenvalues, damping):
    place = jnp.stack([lax.axis_index("example"), lax.axis_index("layer")])

    own, docs = query_grads[0], doc_grads[0]

    docs_other = held(send(docs, dc=1))

    by_y = both_ways(own, "dy")
    near = both_ways(own, "dz")

    row = pack(in_basis[0], eigenvalues[0], out_basis[0])
    twin = send(row, dc=1)
    pair = join([row, twin], by_y)
    column = [send(pair, dy=d) for d in range(1, NY)]
    by_y += far_side(by_y, "dy", column[:1])
    plane = join([pair] + column, [*near, *by_y[2:], docs_other])
    pieces = [plane] + [send(plane, dz=d) for d in range(1, NZ)]
    far = far_side(near, "dz", pieces[1:])

    tables = prepare(place, damping, pieces, [docs_other])

    side = join(near, [])
    side_y = both_ways(side, "dy")
    far = join(far, [])
    far_y = both_ways(far, "dy")
    first = rotate(tables, (own, *by_y), [])
    side_y += far_side(side_y, "dy", [first])
    far_y += far_side(far_y, "dy", [first])

    steps = (0, 1, -1, 2)
    offsets = (
        [(dy, 0) for dy in steps],
        [(dy, dz) for dy in steps for dz in (1, -1)],
        [(dy, 2) for dy in steps],
    )

    def scored(conditioned):
        theirs = send(scores_of(conditioned, docs_other), dc=1)
        return scores_of(conditioned, docs), theirs

    near_parts = scored(first)
    odd_parts = scored(rotate(tables, (side, *side_y), near_parts[:1]))
    odd = arrange(place, offsets[1:2], odd_parts, [])
    odd_waves = spread_over_layers(odd)
    far_parts = scored(rotate(tables, (far, *far_y), [odd]))
    even = arrange(place, offsets[::2], near_parts + far_parts, odd_waves[1:])
    return finish(place, spread_over_layers(even), odd_waves)


def solution(mesh):
    placed = P("layer", "example", None)
    return jax.shard_map(
        body,
        mesh=mesh,
        in_specs=(placed,) * 5 + (P("layer"),),
        out_specs=P("layer", "example"),
        check_vma=False,
    )
```

```python
import functools
import jax
import jax.numpy as jnp
from jax import lax
from jax.experimental import pallas as pl
from jax.experimental.pallas import tpu as pltpu
from jax.sharding import PartitionSpec as P

NY, NZ, NC = 4, 4, 2
NL, NX = 2, 4
ROWS = 32
CHUNK = 7
OUT, IN = 32, 128
F32, BF16 = jnp.float32, jnp.bfloat16
VMEM = pl.BlockSpec(memory_space=pltpu.VMEM)
SMEM = pl.BlockSpec(memory_space=pltpu.SMEM)
ANY = pl.BlockSpec(memory_space=pl.ANY)


def example_shift(dy, dz, dc):
    def place(y, z, c):
        return (y % NY) * NZ * NC + (z % NZ) * NC + c % NC

    return [
        (place(y, z, c), place(y + dy, z + dz, c + dc))
        for y in range(NY)
        for z in range(NZ)
        for c in range(NC)
    ]


def ring_shift(dy, dz):
    def place(y, z, c):
        return (y % NY) * NZ * NC + (z % NZ) * NC + c

    return [
        (place(y, z, c), place(y + dy * (1 - 2 * c), z + dz * (1 - 2 * c), c))
        for y in range(NY)
        for z in range(NZ)
        for c in range(NC)
    ]


def layer_shift(dl, dx):
    return [
        (a * NX + x, ((a + dl) % NL) * NX + (x + dx) % NX) for a in range(NL) for x in range(NX)
    ]


def send(x, dy=0, dz=0, dc=0):
    return lax.ppermute(x, "example", example_shift(dy, dz, dc))


def split2(x):
    high = x.astype(BF16)
    return high, (x - high.astype(F32)).astype(BF16)


def mm(a, b, contract=((1,), (0,))):
    return lax.dot_general(a, b, (contract, ((), ())), preferred_element_type=F32)


def coordinates(example):
    return example >> 3, (example >> 1) & 3, example & 1


def held_kernel(x_ref, *refs):
    pltpu.sync_copy(x_ref, refs[-1])


def held(x, after=()):
    return pl.pallas_call(
        held_kernel,
        out_shape=jax.ShapeDtypeStruct(x.shape, x.dtype),
        in_specs=[ANY] * (1 + len(after)),
        out_specs=VMEM,
        compiler_params=pltpu.CompilerParams(vmem_limit_bytes=16 << 20),
        cost_estimate=pl.CostEstimate(flops=0, bytes_accessed=2 * x.nbytes, transcendentals=0),
        name="held",
    )(x, *after)


def pack_kernel(in_ref, eig_ref, basis_ref, out_ref):
    out_ref[...] = jnp.zeros_like(out_ref)
    out_ref[0:4, :] = in_ref[...]
    out_ref[4:5, :] = eig_ref[...]
    out_ref[5:6, 0:OUT] = basis_ref[...]


def pack(*parts):
    return pl.pallas_call(
        pack_kernel,
        out_shape=jax.ShapeDtypeStruct((8, IN), F32),
        in_specs=[VMEM] * 3,
        out_specs=VMEM,
        compiler_params=pltpu.CompilerParams(vmem_limit_bytes=1 << 20),
        name="pack",
    )(*parts)


def join_kernel(count, *refs):
    parts, out_ref = refs[:count], refs[-1]
    rows = parts[0].shape[0]
    for k, part in enumerate(parts):
        out_ref[rows * k : rows * (k + 1), :] = part[...]


def join(parts, after):
    rows, columns = parts[0].shape
    return pl.pallas_call(
        functools.partial(join_kernel, len(parts)),
        out_shape=jax.ShapeDtypeStruct((rows * len(parts), columns), parts[0].dtype),
        in_specs=[VMEM] * len(parts) + [ANY] * len(after),
        out_specs=VMEM,
        compiler_params=pltpu.CompilerParams(vmem_limit_bytes=4 << 20),
        name="join",
    )(*parts, *after)


def prepare_kernel(place_ref, damp_ref, *refs):
    pieces, rows = refs[:NZ], refs[-1]
    left_ref, right_ref, in_ref, back_ref, scale_ref = refs[-6:-1]
    y, z, c = coordinates(place_ref[0])
    for dz in range(NZ):
        for dy in range(NY):
            for dc in range(NC):
                owner = ((y - dy) & 3) * 8 + ((z - dz) & 3) * 2 + (c ^ dc)
                k = dy * NC + dc
                piece = pieces[dz][8 * k : 8 * k + 8, :]
                rows[pl.ds(pl.multiple_of(owner * 8, 8), 8), :] = piece
    table = rows[...]
    high, low = split2(table)
    lowest = (table - high.astype(F32) - low.astype(F32)).astype(BF16)

    def iota(shape, axis):
        return lax.broadcasted_iota(jnp.int32, shape, axis)

    def pick(condition):
        return condition.astype(F32).astype(BF16)

    r, k = iota((IN, 256), 0), iota((IN, 256), 1)
    pick_in = pick(k == (r // 4) * 8 + r % 4)
    basis, rest = mm(pick_in, high), mm(pick_in, low)
    in_ref[...] = jnp.concatenate([basis, rest], axis=0).astype(BF16)
    turned, turned_rest = basis.T, rest.T
    back_ref[...] = jnp.concatenate(
        [
            jnp.concatenate([turned, turned_rest], axis=1),
            jnp.concatenate([turned, jnp.zeros_like(turned)], axis=1),
        ],
        axis=0,
    ).astype(BF16)
    r, k = iota((256, 256), 0), iota((256, 256), 1)
    pick_eig = pick(k == (r // 8) * 8 + 4)
    eig = mm(pick_eig, high) + (mm(pick_eig, low) + mm(pick_eig, lowest))
    scale_ref[...] = 1.0 / (eig + damp_ref[0])
    pick_out = pick(k == (r // 8) * 8 + 5)
    spread = pick(iota((IN, 256), 0) == iota((IN, 256), 1) // 8)
    same = (r % 8 == k % 8).astype(F32)
    for term, part in enumerate((high, low)):
        whole = mm(mm(pick_out, part).astype(BF16), spread) * same
        right_ref[256 * term : 256 * (term + 1), :] = whole.astype(BF16)
        left_ref[256 * term : 256 * (term + 1), :] = whole.T.astype(BF16)


def prepare(place, damping, pieces, after):
    shape = jax.ShapeDtypeStruct
    return pl.pallas_call(
        prepare_kernel,
        out_shape=(
            shape((512, 256), BF16),
            shape((512, 256), BF16),
            shape((2 * IN, IN), BF16),
            shape((2 * IN, 2 * IN), BF16),
            shape((256, IN), F32),
        ),
        in_specs=[SMEM, SMEM] + [VMEM] * NZ + [ANY] * len(after),
        out_specs=(VMEM,) * 5,
        scratch_shapes=[pltpu.VMEM((256, 128), F32)],
        compiler_params=pltpu.CompilerParams(vmem_limit_bytes=16 << 20),
        cost_estimate=pl.CostEstimate(flops=200_000_000, bytes_accessed=1 << 20, transcendentals=0),
        name="prepare",
    )(place, damping, *pieces, *after)


def mix(matrix, x):
    high, low = split2(x)
    both = mm(matrix, high)
    return both[:256] + (both[256:] + mm(matrix[:256], low))


def rotate_chunk(x, left, right, basis, back, scale):
    count = 2 * len(x)
    tall = jnp.concatenate(
        [piece[:, IN * i : IN * (i + 1)] for piece in x for i in range(OUT)], axis=0
    )
    half = mm(jnp.concatenate([tall, tall], axis=1), basis)
    half = half.reshape(count // 2, OUT, 2, 8, IN)
    side = jnp.concatenate(
        [half[g // 2, :, g % 2].reshape(OUT * 8, IN) for g in range(count)], axis=1
    )
    rotated = mix(left, side)
    scaled = jnp.concatenate(
        [rotated[:, IN * g : IN * (g + 1)] * scale for g in range(count)], axis=0
    )
    restored = mm(jnp.concatenate(split2(scaled), axis=1), back)
    restored = restored[:, :IN] + restored[:, IN:]
    side = jnp.concatenate([restored[256 * g : 256 * (g + 1)] for g in range(count)], axis=1)
    return mix(right, side)


def rotate_kernel(most, count, left_ref, right_ref, in_ref, back_ref, scale_ref, *refs):
    blocks, out_ref = refs[:count], refs[-1]
    pieces = [(b, at) for b in blocks for at in range(0, b.shape[0], 16)]
    step = -(-len(pieces) // -(-len(pieces) // most))
    for first in range(0, len(pieces), step):
        chunk = pieces[first : first + step]
        done = rotate_chunk(
            [b[at : at + 16, :] for b, at in chunk],
            left_ref[...],
            right_ref[...],
            in_ref[...],
            back_ref[...],
            scale_ref[...],
        )
        for p in range(len(chunk)):
            to = 16 * (first + p)
            for i in range(OUT):
                rows = done[8 * i : 8 * i + 8, 2 * IN * p : 2 * IN * (p + 1)]
                rows = jnp.concatenate([rows[:, :IN], rows[:, IN:]], axis=0)
                out_ref[to : to + 16, IN * i : IN * (i + 1)] = rows.astype(BF16)


def rotate(tables, blocks, after):
    rows = sum(b.shape[0] for b in blocks)
    width = blocks[0].shape[1]
    return pl.pallas_call(
        functools.partial(rotate_kernel, CHUNK, len(blocks)),
        out_shape=jax.ShapeDtypeStruct((rows, width), BF16),
        in_specs=[VMEM] * (5 + len(blocks)) + [ANY] * len(after),
        out_specs=VMEM,
        compiler_params=pltpu.CompilerParams(vmem_limit_bytes=32 << 20),
        cost_estimate=pl.CostEstimate(
            flops=rows * 30_000_000, bytes_accessed=4 * rows * width, transcendentals=0
        ),
        name="rotate",
    )(*tables, *blocks, *after)


def scores_of(conditioned, documents):
    return lax.dot_general(
        conditioned, documents, (((1,), (1,)), ((), ())), preferred_element_type=F32
    ).astype(BF16)


def arrange_kernel(offsets, place_ref, *refs):
    parts, out_ref = refs[: 2 * len(offsets)], refs[-1]
    y, z, c = coordinates(place_ref[0])
    layer = place_ref[1]
    for k, part in enumerate(parts):
        kind = c ^ (k % 2)
        way = 1 - 2 * kind
        for at, (dy, dz) in enumerate(offsets[k // 2]):
            from_z = (z - way * dz) & 3
            to = ((y - way * dy) & 3) * 2 + (from_z >> 1)
            turn = ((to ^ layer) & 4) + ((to - layer) & 3)
            out_ref[turn * 4 + (from_z & 1) * 2 + kind] = part[ROWS * at : ROWS * (at + 1), :]


def arrange(place, offsets, parts, after):
    count = sum(p.shape[0] for p in parts) // ROWS
    columns = parts[0].shape[1]
    return pl.pallas_call(
        functools.partial(arrange_kernel, offsets),
        out_shape=jax.ShapeDtypeStruct((count, ROWS, columns), BF16),
        in_specs=[SMEM] + [VMEM] * len(parts) + [ANY] * len(after),
        out_specs=VMEM,
        compiler_params=pltpu.CompilerParams(vmem_limit_bytes=16 << 20),
        cost_estimate=pl.CostEstimate(
            flops=0, bytes_accessed=count * ROWS * columns * 4, transcendentals=0
        ),
        name="arrange",
    )(place, *parts, *after)


def finish_kernel(*refs):
    total = refs[0][...].astype(F32)
    for part in refs[1:-1]:
        total += part[...].astype(F32)
    refs[-1][...] = total


def finish(parts):
    return pl.pallas_call(
        finish_kernel,
        out_shape=jax.ShapeDtypeStruct(parts[0].shape, F32),
        in_specs=[VMEM] * len(parts),
        out_specs=VMEM,
        compiler_params=pltpu.CompilerParams(vmem_limit_bytes=8 << 20),
        name="finish",
    )(*parts)


def spread_over_layers(ready):
    ready = ready.reshape(NL * NX, 4 * ROWS, ready.shape[-1])
    parts = [ready[0]]
    for dl in range(NL):
        for dx in range(NX):
            if dl or dx:
                parts.append(lax.ppermute(ready[dl * NX + dx], "layer", layer_shift(dl, dx)))
    return parts


def ring(x, dy=0, dz=0):
    return lax.ppermute(x, "example", ring_shift(dy, dz))


def body(query_grads, doc_grads, out_basis, in_basis, eigenvalues, damping):
    place = jnp.stack([lax.axis_index("example"), lax.axis_index("layer")])

    own, docs = query_grads[0], doc_grads[0]

    docs_other = held(send(docs, dc=1))

    y1 = ring(own, dy=1)
    row = pack(in_basis[0], eigenvalues[0], out_basis[0])
    twin = send(row, dc=1)
    z1 = join([ring(own, dz=1)], [twin])
    y2 = ring(y1, dy=1)
    pair = join([row, twin], [])
    column = [send(pair, dy=d) for d in range(1, NY)]
    z2 = join([ring(z1, dz=1)], column)
    y3 = ring(y2, dy=1)
    plane = join([pair] + column, [docs_other])
    pieces = [plane] + [send(plane, dz=d) for d in range(1, NZ)]
    z3 = ring(z2, dz=1)

    side = join([z1, z2, z3], [plane, y3])
    tables = prepare(place, damping, pieces, [])
    side1 = join([ring(side, dy=1)], tables[-1:])
    side2 = ring(side1, dy=1)
    side3 = ring(side2, dy=1)

    offsets = [[(dy, 0) for dy in range(NY)] + [(0, dz) for dz in range(1, NZ)]]
    offsets += [[(dy, dz) for dz in range(1, NZ)] for dy in range(1, NY)]
    parts, after = [], []
    for blocks in ((own, y1, y2, y3, side), (side1,), (side2,), (side3,)):
        conditioned = rotate(tables, blocks, after)
        theirs = send(scores_of(conditioned, docs_other), dc=1)
        parts += [scores_of(conditioned, docs), theirs]
        after = parts[-2:-1]
    ready = arrange(place, offsets, parts, [])
    return finish(spread_over_layers(ready))


def solution(mesh):
    placed = P("layer", "example", None)
    return jax.shard_map(
        body,
        mesh=mesh,
        in_specs=(placed,) * 5 + (P("layer"),),
        out_specs=P("layer", "example"),
        check_vma=False,
    )
```

```python
import functools
import jax
import jax.numpy as jnp
from jax import lax
from jax.experimental import pallas as pl
from jax.experimental.pallas import tpu as pltpu
from jax.sharding import PartitionSpec as P

NY, NZ, NC = 4, 4, 2
NL, NX = 2, 4
ROWS = 32
CHUNK = 7
OUT, IN = 32, 128
F32, BF16 = jnp.float32, jnp.bfloat16
VMEM = pl.BlockSpec(memory_space=pltpu.VMEM)
SMEM = pl.BlockSpec(memory_space=pltpu.SMEM)
ANY = pl.BlockSpec(memory_space=pl.ANY)


def example_shift(dy, dz, dc):
    def place(y, z, c):
        return (y % NY) * NZ * NC + (z % NZ) * NC + c % NC

    return [
        (place(y, z, c), place(y + dy, z + dz, c + dc))
        for y in range(NY)
        for z in range(NZ)
        for c in range(NC)
    ]


def layer_shift(dl, dx):
    return [
        (a * NX + x, ((a + dl) % NL) * NX + (x + dx) % NX) for a in range(NL) for x in range(NX)
    ]


def send(x, dy=0, dz=0, dc=0):
    return lax.ppermute(x, "example", example_shift(dy, dz, dc))


def split2(x):
    high = x.astype(BF16)
    return high, (x - high.astype(F32)).astype(BF16)


def mm(a, b, contract=((1,), (0,))):
    return lax.dot_general(a, b, (contract, ((), ())), preferred_element_type=F32)


def coordinates(example):
    return example >> 3, (example >> 1) & 3, example & 1


def held_kernel(x_ref, *refs):
    pltpu.sync_copy(x_ref, refs[-1])


def held(x, after=()):
    return pl.pallas_call(
        held_kernel,
        out_shape=jax.ShapeDtypeStruct(x.shape, x.dtype),
        in_specs=[ANY] * (1 + len(after)),
        out_specs=VMEM,
        compiler_params=pltpu.CompilerParams(vmem_limit_bytes=16 << 20),
        cost_estimate=pl.CostEstimate(flops=0, bytes_accessed=2 * x.nbytes, transcendentals=0),
        name="held",
    )(x, *after)


def pack_kernel(in_ref, eig_ref, basis_ref, out_ref, in_rows, eig_rows, basis_rows, sems):
    copies = [
        pltpu.make_async_copy(source, target, sems.at[k])
        for k, (source, target) in enumerate(
            ((in_ref, in_rows), (eig_ref, eig_rows), (basis_ref, basis_rows))
        )
    ]
    for copy in copies:
        copy.start()
    out_ref[...] = jnp.zeros_like(out_ref)
    for copy in copies:
        copy.wait()
    out_ref[0:4, :] = in_rows[...]
    out_ref[4:5, :] = eig_rows[...]
    out_ref[5:6, 0:OUT] = basis_rows[...]


def pack(*parts):
    return pl.pallas_call(
        pack_kernel,
        out_shape=jax.ShapeDtypeStruct((8, IN), F32),
        in_specs=[ANY] * 3,
        out_specs=VMEM,
        scratch_shapes=[pltpu.VMEM(p.shape, p.dtype) for p in parts]
        + [pltpu.SemaphoreType.DMA((3,))],
        compiler_params=pltpu.CompilerParams(vmem_limit_bytes=56 << 20),
        name="pack",
    )(*parts)


def join_kernel(count, *refs):
    parts, out_ref = refs[:count], refs[-1]
    at = 0
    for part in parts:
        out_ref[at : at + part.shape[0], :] = part[...]
        at += part.shape[0]


def join(parts, after):
    rows, columns = sum(p.shape[0] for p in parts), parts[0].shape[1]
    return pl.pallas_call(
        functools.partial(join_kernel, len(parts)),
        out_shape=jax.ShapeDtypeStruct((rows, columns), parts[0].dtype),
        in_specs=[VMEM] * len(parts) + [ANY] * len(after),
        out_specs=VMEM,
        compiler_params=pltpu.CompilerParams(vmem_limit_bytes=4 << 20),
        name="join",
    )(*parts, *after)


def prepare_kernel(place_ref, damp_ref, *refs):
    pieces, rows = refs[:NZ], refs[-1]
    left_ref, right_ref, in_ref, back_ref, scale_ref = refs[-6:-1]
    y, z, c = coordinates(place_ref[0])
    for dz in range(NZ):
        for dy in range(NY):
            for dc in range(NC):
                owner = ((y - dy) & 3) * 8 + ((z - dz) & 3) * 2 + (c ^ dc)
                k = dy * NC + dc
                piece = pieces[dz][8 * k : 8 * k + 8, :]
                rows[pl.ds(pl.multiple_of(owner * 8, 8), 8), :] = piece
    table = rows[...]
    high, low = split2(table)
    lowest = (table - high.astype(F32) - low.astype(F32)).astype(BF16)

    def iota(shape, axis):
        return lax.broadcasted_iota(jnp.int32, shape, axis)

    def pick(condition):
        return condition.astype(F32).astype(BF16)

    r, k = iota((IN, 256), 0), iota((IN, 256), 1)
    pick_in = pick(k == (r // 4) * 8 + r % 4)
    basis, rest = mm(pick_in, high), mm(pick_in, low)
    in_ref[...] = jnp.concatenate([basis, rest], axis=0).astype(BF16)
    turned, turned_rest = basis.T, rest.T
    back_ref[...] = jnp.concatenate(
        [
            jnp.concatenate([turned, turned_rest], axis=1),
            jnp.concatenate([turned, jnp.zeros_like(turned)], axis=1),
        ],
        axis=0,
    ).astype(BF16)
    r, k = iota((256, 256), 0), iota((256, 256), 1)
    pick_eig = pick(k == (r // 8) * 8 + 4)
    eig = mm(pick_eig, high) + (mm(pick_eig, low) + mm(pick_eig, lowest))
    scale_ref[...] = 1.0 / (eig + damp_ref[0])
    pick_out = pick(k == (r // 8) * 8 + 5)
    spread = pick(iota((IN, 256), 0) == iota((IN, 256), 1) // 8)
    same = (r % 8 == k % 8).astype(F32)
    for term, part in enumerate((high, low)):
        whole = mm(mm(pick_out, part).astype(BF16), spread) * same
        right_ref[256 * term : 256 * (term + 1), :] = whole.astype(BF16)
        left_ref[256 * term : 256 * (term + 1), :] = whole.T.astype(BF16)


def prepare(place, damping, pieces, after):
    shape = jax.ShapeDtypeStruct
    return pl.pallas_call(
        prepare_kernel,
        out_shape=(
            shape((512, 256), BF16),
            shape((512, 256), BF16),
            shape((2 * IN, IN), BF16),
            shape((2 * IN, 2 * IN), BF16),
            shape((256, IN), F32),
        ),
        in_specs=[SMEM, SMEM] + [VMEM] * NZ + [ANY] * len(after),
        out_specs=(VMEM,) * 5,
        scratch_shapes=[pltpu.VMEM((256, 128), F32)],
        compiler_params=pltpu.CompilerParams(vmem_limit_bytes=16 << 20),
        cost_estimate=pl.CostEstimate(flops=200_000_000, bytes_accessed=1 << 20, transcendentals=0),
        name="prepare",
    )(place, damping, *pieces, *after)


def mix(matrix, x):
    high, low = split2(x)
    both = mm(matrix, high)
    return both[:256] + (both[256:] + mm(matrix[:256], low))


def rotate_chunk(x, left, right, basis, back, scale):
    count = 2 * len(x)
    tall = jnp.concatenate(
        [piece[:, IN * i : IN * (i + 1)] for piece in x for i in range(OUT)], axis=0
    )
    half = mm(jnp.concatenate([tall, tall], axis=1), basis)
    half = half.reshape(count // 2, OUT, 2, 8, IN)
    side = jnp.concatenate(
        [half[g // 2, :, g % 2].reshape(OUT * 8, IN) for g in range(count)], axis=1
    )
    rotated = mix(left, side)
    scaled = jnp.concatenate(
        [rotated[:, IN * g : IN * (g + 1)] * scale for g in range(count)], axis=0
    )
    restored = mm(jnp.concatenate(split2(scaled), axis=1), back)
    restored = restored[:, :IN] + restored[:, IN:]
    side = jnp.concatenate([restored[256 * g : 256 * (g + 1)] for g in range(count)], axis=1)
    return mix(right, side)


def rotate_kernel(most, count, left_ref, right_ref, in_ref, back_ref, scale_ref, *refs):
    blocks, out_ref = refs[:count], refs[-1]
    pieces = [(b, at) for b in blocks for at in range(0, b.shape[0], 16)]
    step = -(-len(pieces) // -(-len(pieces) // most))
    for first in range(0, len(pieces), step):
        chunk = pieces[first : first + step]
        done = rotate_chunk(
            [b[at : at + 16, :] for b, at in chunk],
            left_ref[...],
            right_ref[...],
            in_ref[...],
            back_ref[...],
            scale_ref[...],
        )
        for p in range(len(chunk)):
            to = 16 * (first + p)
            for i in range(OUT):
                rows = done[8 * i : 8 * i + 8, 2 * IN * p : 2 * IN * (p + 1)]
                rows = jnp.concatenate([rows[:, :IN], rows[:, IN:]], axis=0)
                out_ref[to : to + 16, IN * i : IN * (i + 1)] = rows.astype(BF16)


def rotate(tables, blocks, after):
    rows = sum(b.shape[0] for b in blocks)
    width = blocks[0].shape[1]
    return pl.pallas_call(
        functools.partial(rotate_kernel, CHUNK, len(blocks)),
        out_shape=jax.ShapeDtypeStruct((rows, width), BF16),
        in_specs=[VMEM] * (5 + len(blocks)) + [ANY] * len(after),
        out_specs=VMEM,
        compiler_params=pltpu.CompilerParams(vmem_limit_bytes=32 << 20),
        cost_estimate=pl.CostEstimate(
            flops=rows * 30_000_000, bytes_accessed=4 * rows * width, transcendentals=0
        ),
        name="rotate",
    )(*tables, *blocks, *after)


def scores_of(conditioned, documents):
    return lax.dot_general(
        conditioned, documents, (((1,), (1,)), ((), ())), preferred_element_type=F32
    ).astype(BF16)


def arrange_kernel(offsets, place_ref, *refs):
    parts, out_ref = refs[: 2 * len(offsets)], refs[-1]
    y, z, c = coordinates(place_ref[0])
    layer = place_ref[1]
    for k, part in enumerate(parts):
        kind = c ^ (k % 2)
        for at, (dy, dz) in enumerate(offsets[k // 2]):
            from_z = (z - dz) & 3
            to = ((y - dy) & 3) * 2 + (from_z >> 1)
            turn = ((to ^ layer) & 4) + ((to - layer) & 3)
            out_ref[turn * 4 + (from_z & 1) * 2 + kind] = part[ROWS * at : ROWS * (at + 1), :]


def arrange(place, offsets, parts, after):
    count = sum(p.shape[0] for p in parts) // ROWS
    columns = parts[0].shape[1]
    return pl.pallas_call(
        functools.partial(arrange_kernel, offsets),
        out_shape=jax.ShapeDtypeStruct((count, ROWS, columns), BF16),
        in_specs=[SMEM] + [VMEM] * len(parts) + [ANY] * len(after),
        out_specs=VMEM,
        compiler_params=pltpu.CompilerParams(vmem_limit_bytes=16 << 20),
        cost_estimate=pl.CostEstimate(
            flops=0, bytes_accessed=count * ROWS * columns * 4, transcendentals=0
        ),
        name="arrange",
    )(place, *parts, *after)


def finish_kernel(*refs):
    total = refs[0][...].astype(F32)
    for part in refs[1:-1]:
        total += part[...].astype(F32)
    refs[-1][...] = total


def finish(parts):
    return pl.pallas_call(
        finish_kernel,
        out_shape=jax.ShapeDtypeStruct(parts[0].shape, F32),
        in_specs=[VMEM] * len(parts),
        out_specs=VMEM,
        compiler_params=pltpu.CompilerParams(vmem_limit_bytes=8 << 20),
        name="finish",
    )(*parts)


def spread_over_layers(ready):
    ready = ready.reshape(NL * NX, 4 * ROWS, ready.shape[-1])
    parts = [ready[0]]
    for dl, dx in ((1, 2), (0, 2), (1, 1), (1, 3), (1, 0), (0, 1), (0, 3)):
        parts.append(lax.ppermute(ready[dl * NX + dx], "layer", layer_shift(dl, dx)))
    return parts


def halves_kernel(behind_ref, ahead_ref, *refs):
    first_ref, second_ref = refs[-2:]
    rows = first_ref.shape[0]
    first_ref[...] = behind_ref[:rows, :]
    second_ref[...] = ahead_ref[rows:, :]


def halves(behind, ahead, after):
    rows, columns = behind.shape
    return pl.pallas_call(
        halves_kernel,
        out_shape=(jax.ShapeDtypeStruct((rows // 2, columns), behind.dtype),) * 2,
        in_specs=[VMEM, VMEM] + [ANY] * len(after),
        out_specs=(VMEM, VMEM),
        compiler_params=pltpu.CompilerParams(vmem_limit_bytes=4 << 20),
        name="halves",
    )(behind, ahead, *after)


def both_ways(own, axis):
    return send(own, **{axis: 1}), send(own, **{axis: -1})


def far_side(near, axis, after=()):
    first, second = halves(*near, after)
    return send(first, **{axis: 1}), send(second, **{axis: -1})


def body(query_grads, doc_grads, out_basis, in_basis, eigenvalues, damping):
    place = jnp.stack([lax.axis_index("example"), lax.axis_index("layer")])

    own, docs = query_grads[0], doc_grads[0]

    docs_other = held(send(docs, dc=1))

    near = both_ways(own, "dz")
    by_y = both_ways(own, "dy")
    row = pack(in_basis[0], eigenvalues[0], out_basis[0])
    pair = join([row, send(row, dc=1)], [*by_y, docs_other])
    column = [send(pair, dy=d) for d in range(1, NY)]
    far = far_side(near, "dz")
    by_y += far_side(by_y, "dy", column)

    side = join([*near, *far], [])
    side_y = both_ways(side, "dy")
    plane = join([pair] + column, by_y[2:])
    pieces = [plane] + [send(plane, dz=d) for d in range(1, NZ)]
    tables = prepare(place, damping, pieces, [])

    offsets = (
        [(0, 0), (1, 0), (-1, 0), (2, 0), (0, 1), (0, -1), (0, 2)],
        [(dy, dz) for dy in (1, -1) for dz in (1, -1, 2)],
        [(2, dz) for dz in (1, -1, 2)],
    )
    first = rotate(tables, (own, *by_y, side), [])
    side_far = far_side(side_y, "dy", [first])

    def scored(conditioned):
        theirs = send(scores_of(conditioned, docs_other), dc=1)
        return [scores_of(conditioned, docs), theirs]

    parts = scored(first)
    parts += scored(rotate(tables, side_y, parts[:1]))
    parts += scored(rotate(tables, side_far, parts[2:3]))
    return finish(spread_over_layers(arrange(place, offsets, parts, [])))


def solution(mesh):
    placed = P("layer", "example", None)
    return jax.shard_map(
        body,
        mesh=mesh,
        in_specs=(placed,) * 5 + (P("layer"),),
        out_specs=P("layer", "example"),
        check_vma=False,
    )
```

```python
import functools
import jax
import jax.numpy as jnp
from jax import lax
from jax.experimental import pallas as pl
from jax.experimental.pallas import tpu as pltpu
from jax.sharding import PartitionSpec as P

NY, NZ, NC = 4, 4, 2
NL, NX = 2, 4
ROWS = 32
CHUNK = 8
OUT, IN = 32, 128
F32, BF16 = jnp.float32, jnp.bfloat16
VMEM = pl.BlockSpec(memory_space=pltpu.VMEM)
SMEM = pl.BlockSpec(memory_space=pltpu.SMEM)
ANY = pl.BlockSpec(memory_space=pl.ANY)
HBM = pl.BlockSpec(memory_space=pltpu.HBM)


def example_shift(dy, dz, dc):
    def place(y, z, c):
        return (y % NY) * NZ * NC + (z % NZ) * NC + c % NC

    return [
        (place(y, z, c), place(y + dy, z + dz, c + dc))
        for y in range(NY)
        for z in range(NZ)
        for c in range(NC)
    ]


def layer_shift(dl, dx):
    return [
        (a * NX + x, ((a + dl) % NL) * NX + (x + dx) % NX) for a in range(NL) for x in range(NX)
    ]


def send(x, dy=0, dz=0, dc=0):
    return lax.ppermute(x, "example", example_shift(dy, dz, dc))


def split2(x):
    high = x.astype(BF16)
    return high, (x - high.astype(F32)).astype(BF16)


def mm(a, b, contract=((1,), (0,))):
    return lax.dot_general(a, b, (contract, ((), ())), preferred_element_type=F32)


def coordinates(example):
    return example >> 3, (example >> 1) & 3, example & 1


def held_kernel(x_ref, *refs):
    pltpu.sync_copy(x_ref, refs[-1])


def held(x, after=()):
    return pl.pallas_call(
        held_kernel,
        out_shape=jax.ShapeDtypeStruct(x.shape, x.dtype),
        in_specs=[HBM] + [ANY] * len(after),
        out_specs=VMEM,
        compiler_params=pltpu.CompilerParams(vmem_limit_bytes=16 << 20),
        cost_estimate=pl.CostEstimate(flops=0, bytes_accessed=2 * x.nbytes, transcendentals=0),
        name="held",
    )(x, *after)


def pack_kernel(in_ref, eig_ref, basis_ref, out_ref, in_rows, eig_rows, basis_rows, sems):
    copies = [
        pltpu.make_async_copy(source, target, sems.at[k])
        for k, (source, target) in enumerate(
            ((in_ref, in_rows), (eig_ref, eig_rows), (basis_ref, basis_rows))
        )
    ]
    for copy in copies:
        copy.start()
    out_ref[...] = jnp.zeros_like(out_ref)
    for copy in copies:
        copy.wait()
    out_ref[0:4, :] = in_rows[...]
    out_ref[4:5, :] = eig_rows[...]
    out_ref[5:6, 0:OUT] = basis_rows[...]


def pack(*parts):
    return pl.pallas_call(
        pack_kernel,
        out_shape=jax.ShapeDtypeStruct((8, IN), F32),
        in_specs=[HBM] * 3,
        out_specs=VMEM,
        scratch_shapes=[pltpu.VMEM(p.shape, p.dtype) for p in parts]
        + [pltpu.SemaphoreType.DMA((3,))],
        compiler_params=pltpu.CompilerParams(vmem_limit_bytes=1 << 20),
        name="pack",
    )(*parts)


def join_kernel(count, *refs):
    parts, out_ref = refs[:count], refs[-1]
    at = 0
    for part in parts:
        out_ref[at : at + part.shape[0], :] = part[...]
        at += part.shape[0]


def join(parts, after):
    rows, columns = sum(p.shape[0] for p in parts), parts[0].shape[1]
    return pl.pallas_call(
        functools.partial(join_kernel, len(parts)),
        out_shape=jax.ShapeDtypeStruct((rows, columns), parts[0].dtype),
        in_specs=[VMEM] * len(parts) + [ANY] * len(after),
        out_specs=VMEM,
        compiler_params=pltpu.CompilerParams(vmem_limit_bytes=4 << 20),
        name="join",
    )(*parts, *after)


def prepare_kernel(place_ref, damp_ref, *refs):
    pieces, rows = refs[:NZ], refs[-1]
    left_ref, right_ref, in_ref, back_ref, scale_ref = refs[-6:-1]
    y, z, c = coordinates(place_ref[0])
    for dz in range(NZ):
        for dy in range(NY):
            for dc in range(NC):
                owner = ((y - dy) & 3) * 8 + ((z - dz) & 3) * 2 + (c ^ dc)
                k = dy * NC + dc
                piece = pieces[dz][8 * k : 8 * k + 8, :]
                rows[pl.ds(pl.multiple_of(owner * 8, 8), 8), :] = piece
    table = rows[...]
    high, low = split2(table)
    lowest = (table - high.astype(F32) - low.astype(F32)).astype(BF16)

    def iota(shape, axis):
        return lax.broadcasted_iota(jnp.int32, shape, axis)

    def pick(condition):
        return condition.astype(F32).astype(BF16)

    r, k = iota((IN, 256), 0), iota((IN, 256), 1)
    pick_in = pick(k == (r // 4) * 8 + r % 4)
    basis, rest = mm(pick_in, high), mm(pick_in, low)
    in_ref[...] = jnp.concatenate([basis, rest], axis=0).astype(BF16)
    turned, turned_rest = basis.T, rest.T
    back_ref[...] = jnp.concatenate(
        [
            jnp.concatenate([turned, turned_rest], axis=1),
            jnp.concatenate([turned, jnp.zeros_like(turned)], axis=1),
        ],
        axis=0,
    ).astype(BF16)
    r, k = iota((256, 256), 0), iota((256, 256), 1)
    pick_eig = pick(k == (r // 8) * 8 + 4)
    eig = mm(pick_eig, high) + (mm(pick_eig, low) + mm(pick_eig, lowest))
    scale_ref[...] = 1.0 / (eig + damp_ref[0])
    pick_out = pick(k == (r // 8) * 8 + 5)
    spread = pick(iota((IN, 256), 0) == iota((IN, 256), 1) // 8)
    same = (r % 8 == k % 8).astype(F32)
    for term, part in enumerate((high, low)):
        whole = mm(mm(pick_out, part).astype(BF16), spread) * same
        right_ref[256 * term : 256 * (term + 1), :] = whole.astype(BF16)
        left_ref[256 * term : 256 * (term + 1), :] = whole.T.astype(BF16)


def prepare(place, damping, pieces, after):
    shape = jax.ShapeDtypeStruct
    return pl.pallas_call(
        prepare_kernel,
        out_shape=(
            shape((512, 256), BF16),
            shape((512, 256), BF16),
            shape((2 * IN, IN), BF16),
            shape((2 * IN, 2 * IN), BF16),
            shape((256, IN), F32),
        ),
        in_specs=[SMEM, SMEM] + [VMEM] * NZ + [ANY] * len(after),
        out_specs=(VMEM,) * 5,
        scratch_shapes=[pltpu.VMEM((256, 128), F32)],
        compiler_params=pltpu.CompilerParams(vmem_limit_bytes=16 << 20),
        cost_estimate=pl.CostEstimate(flops=200_000_000, bytes_accessed=1 << 20, transcendentals=0),
        name="prepare",
    )(place, damping, *pieces, *after)


def mix(matrix, x):
    high, low = split2(x)
    both = mm(matrix, high)
    return both[:256] + (both[256:] + mm(matrix[:256], low))


def rotate_chunk(x, left, right, basis, back, scale):
    count = 2 * len(x)
    tall = jnp.concatenate(
        [piece[:, IN * i : IN * (i + 1)] for piece in x for i in range(OUT)], axis=0
    )
    half = mm(jnp.concatenate([tall, tall], axis=1), basis)
    half = half.reshape(count // 2, OUT, 2, 8, IN)
    side = jnp.concatenate(
        [half[g // 2, :, g % 2].reshape(OUT * 8, IN) for g in range(count)], axis=1
    )
    rotated = mix(left, side)
    scaled = jnp.concatenate(
        [rotated[:, IN * g : IN * (g + 1)] * scale for g in range(count)], axis=0
    )
    restored = mm(jnp.concatenate(split2(scaled), axis=1), back)
    restored = restored[:, :IN] + restored[:, IN:]
    side = jnp.concatenate([restored[256 * g : 256 * (g + 1)] for g in range(count)], axis=1)
    return mix(right, side)


def rotate_kernel(most, count, left_ref, right_ref, in_ref, back_ref, scale_ref, *refs):
    blocks, out_ref = refs[:count], refs[-1]
    pieces = [(b, at) for b in blocks for at in range(0, b.shape[0], 16)]
    step = -(-len(pieces) // -(-len(pieces) // most))
    for first in range(0, len(pieces), step):
        chunk = pieces[first : first + step]
        done = rotate_chunk(
            [b[at : at + 16, :] for b, at in chunk],
            left_ref[...],
            right_ref[...],
            in_ref[...],
            back_ref[...],
            scale_ref[...],
        )
        for p in range(len(chunk)):
            to = 16 * (first + p)
            for i in range(OUT):
                rows = done[8 * i : 8 * i + 8, 2 * IN * p : 2 * IN * (p + 1)]
                rows = jnp.concatenate([rows[:, :IN], rows[:, IN:]], axis=0)
                out_ref[to : to + 16, IN * i : IN * (i + 1)] = rows.astype(BF16)


def rotate(tables, blocks, after):
    rows = sum(b.shape[0] for b in blocks)
    width = blocks[0].shape[1]
    return pl.pallas_call(
        functools.partial(rotate_kernel, CHUNK, len(blocks)),
        out_shape=jax.ShapeDtypeStruct((rows, width), BF16),
        in_specs=[VMEM] * (5 + len(blocks)) + [ANY] * len(after),
        out_specs=VMEM,
        compiler_params=pltpu.CompilerParams(vmem_limit_bytes=32 << 20),
        cost_estimate=pl.CostEstimate(flops=0, bytes_accessed=0, transcendentals=0),
        name="rotate",
    )(*tables, *blocks, *after)


def scores_of(conditioned, documents):
    return lax.dot_general(
        conditioned, documents, (((1,), (1,)), ((), ())), preferred_element_type=F32
    ).astype(BF16)


def arrange_kernel(offsets, place_ref, *refs):
    parts, out_ref = refs[: 2 * len(offsets)], refs[-1]
    y, z, c = coordinates(place_ref[0])
    layer = place_ref[1]
    for k, part in enumerate(parts):
        kind = c ^ (k % 2)
        for at, (dy, dz) in enumerate(offsets[k // 2]):
            from_z = (z - dz) & 3
            to = ((y - dy) & 3) * 2 + (from_z >> 1)
            turn = ((to ^ layer) & 4) + ((to - layer) & 3)
            out_ref[turn * 4 + (from_z & 1) * 2 + kind] = part[ROWS * at : ROWS * (at + 1), :]


def arrange(place, offsets, parts, after):
    count = sum(p.shape[0] for p in parts) // ROWS
    columns = parts[0].shape[1]
    return pl.pallas_call(
        functools.partial(arrange_kernel, offsets),
        out_shape=jax.ShapeDtypeStruct((count, ROWS, columns), BF16),
        in_specs=[SMEM] + [VMEM] * len(parts) + [ANY] * len(after),
        out_specs=VMEM,
        compiler_params=pltpu.CompilerParams(vmem_limit_bytes=16 << 20),
        cost_estimate=pl.CostEstimate(
            flops=0, bytes_accessed=count * ROWS * columns * 4, transcendentals=0
        ),
        name="arrange",
    )(place, *parts, *after)


def finish_kernel(*refs):
    total = refs[0][...].astype(F32)
    for part in refs[1:-1]:
        total += part[...].astype(F32)
    refs[-1][...] = total


def finish(parts):
    return pl.pallas_call(
        finish_kernel,
        out_shape=jax.ShapeDtypeStruct(parts[0].shape, F32),
        in_specs=[VMEM] * len(parts),
        out_specs=VMEM,
        compiler_params=pltpu.CompilerParams(vmem_limit_bytes=8 << 20),
        name="finish",
    )(*parts)


def spread_over_layers(ready):
    ready = ready.reshape(NL * NX, 4 * ROWS, ready.shape[-1])
    parts = [ready[0]]
    for dl, dx in ((1, 2), (0, 2), (1, 1), (1, 3), (1, 0), (0, 1), (0, 3)):
        parts.append(lax.ppermute(ready[dl * NX + dx], "layer", layer_shift(dl, dx)))
    return parts


def halves_kernel(behind_ref, ahead_ref, *refs):
    first_ref, second_ref = refs[-2:]
    rows = first_ref.shape[0]
    first_ref[...] = behind_ref[:rows, :]
    second_ref[...] = ahead_ref[rows:, :]


def halves(behind, ahead, after):
    rows, columns = behind.shape
    return pl.pallas_call(
        halves_kernel,
        out_shape=(jax.ShapeDtypeStruct((rows // 2, columns), behind.dtype),) * 2,
        in_specs=[VMEM, VMEM] + [ANY] * len(after),
        out_specs=(VMEM, VMEM),
        compiler_params=pltpu.CompilerParams(vmem_limit_bytes=4 << 20),
        name="halves",
    )(behind, ahead, *after)


def both_ways(own, axis):
    return send(own, **{axis: 1}), send(own, **{axis: -1})


def body(query_grads, doc_grads, out_basis, in_basis, eigenvalues, damping):
    place = jnp.stack([lax.axis_index("example"), lax.axis_index("layer")])

    own, docs = query_grads[0], doc_grads[0]
    docs_there = send(docs, dc=1)

    near = both_ways(own, "dz")
    row = pack(in_basis[0], eigenvalues[0], out_basis[0])
    pair = join([row, send(row, dc=1)], [])
    column = [send(pair, dy=d) for d in range(1, NY)]
    plane = join([pair] + column, [docs_there])
    pieces = [plane] + [send(plane, dz=d) for d in range(1, NZ)]
    cut = halves(*near, column)
    far = send(cut[0], dz=1), send(cut[1], dz=-1)
    tables = prepare(place, damping, pieces, [])

    side = join([own, *near, *far], [])
    side_y = both_ways(side, "dy")

    offsets = [[(dy, dz) for dy in group for dz in (0, 1, -1, 2)] for group in ((0,), (1, -1), (2,))]

    first = rotate(tables, (side,), [])
    docs_other = held(docs_there, [first])

    def scored(conditioned):
        theirs = send(scores_of(conditioned, docs_other), dc=1)
        return [scores_of(conditioned, docs), theirs]

    parts = scored(first)
    cut = halves(*side_y, [first])
    side_far = send(cut[0], dy=1), send(cut[1], dy=-1)
    parts += scored(rotate(tables, side_y, [cut[0], parts[0]]))
    parts += scored(rotate(tables, side_far, parts[2:3]))
    return finish(spread_over_layers(arrange(place, offsets, parts, [])))


def solution(mesh):
    placed = P("layer", "example", None)
    return jax.shard_map(
        body,
        mesh=mesh,
        in_specs=(placed,) * 5 + (P("layer"),),
        out_specs=P("layer", "example"),
        check_vma=False,
    )
```

```python
import functools
import jax
import jax.numpy as jnp
from jax import lax
from jax.experimental import pallas as pl
from jax.experimental.pallas import tpu as pltpu
from jax.sharding import PartitionSpec as P

NY, NZ, NC = 4, 4, 2
NL, NX = 2, 4
ROWS = 32
CHUNK = 8
OUT, IN = 32, 128
F32, BF16 = jnp.float32, jnp.bfloat16
VMEM = pl.BlockSpec(memory_space=pltpu.VMEM)
SMEM = pl.BlockSpec(memory_space=pltpu.SMEM)
ANY = pl.BlockSpec(memory_space=pl.ANY)
HBM = pl.BlockSpec(memory_space=pltpu.HBM)


def example_shift(dy, dz, dc):
    def place(y, z, c):
        return (y % NY) * NZ * NC + (z % NZ) * NC + c % NC

    return [
        (place(y, z, c), place(y + dy, z + dz, c + dc))
        for y in range(NY)
        for z in range(NZ)
        for c in range(NC)
    ]


def layer_shift(dl, dx):
    return [
        (a * NX + x, ((a + dl) % NL) * NX + (x + dx) % NX) for a in range(NL) for x in range(NX)
    ]


def send(x, dy=0, dz=0, dc=0):
    return lax.ppermute(x, "example", example_shift(dy, dz, dc))


def split2(x):
    high = x.astype(BF16)
    return high, (x - high.astype(F32)).astype(BF16)


def mm(a, b, contract=((1,), (0,))):
    return lax.dot_general(a, b, (contract, ((), ())), preferred_element_type=F32)


def coordinates(example):
    return example >> 3, (example >> 1) & 3, example & 1


def held_kernel(x_ref, *refs):
    pltpu.sync_copy(x_ref, refs[-1])


def held(x, after=()):
    return pl.pallas_call(
        held_kernel,
        out_shape=jax.ShapeDtypeStruct(x.shape, x.dtype),
        in_specs=[HBM] + [ANY] * len(after),
        out_specs=VMEM,
        compiler_params=pltpu.CompilerParams(vmem_limit_bytes=16 << 20),
        cost_estimate=pl.CostEstimate(flops=0, bytes_accessed=2 * x.nbytes, transcendentals=0),
        name="held",
    )(x, *after)


def pack_kernel(in_ref, eig_ref, basis_ref, out_ref, in_rows, eig_rows, basis_rows, sems):
    copies = [
        pltpu.make_async_copy(source, target, sems.at[k])
        for k, (source, target) in enumerate(
            ((in_ref, in_rows), (eig_ref, eig_rows), (basis_ref, basis_rows))
        )
    ]
    for copy in copies:
        copy.start()
    out_ref[...] = jnp.zeros_like(out_ref)
    for copy in copies:
        copy.wait()
    out_ref[0:4, :] = in_rows[...]
    out_ref[4:5, :] = eig_rows[...]
    out_ref[5:6, 0:OUT] = basis_rows[...]


def pack(*parts):
    return pl.pallas_call(
        pack_kernel,
        out_shape=jax.ShapeDtypeStruct((8, IN), F32),
        in_specs=[HBM] * 3,
        out_specs=VMEM,
        scratch_shapes=[pltpu.VMEM(p.shape, p.dtype) for p in parts]
        + [pltpu.SemaphoreType.DMA((3,))],
        compiler_params=pltpu.CompilerParams(vmem_limit_bytes=1 << 20),
        name="pack",
    )(*parts)


def join_kernel(ranges, *refs):
    out_ref, at = refs[-1], 0
    for part, (low, high) in zip(refs, ranges):
        out_ref[at : at + high - low, :] = part[low:high, :]
        at += high - low


def join(parts, after, ranges=None):
    ranges = ranges or [(0, p.shape[0]) for p in parts]
    rows = sum(high - low for low, high in ranges)
    columns, dtype = parts[0].shape[1], parts[0].dtype
    return pl.pallas_call(
        functools.partial(join_kernel, ranges),
        out_shape=jax.ShapeDtypeStruct((rows, columns), dtype),
        in_specs=[VMEM] * len(parts) + [ANY] * len(after),
        out_specs=VMEM,
        compiler_params=pltpu.CompilerParams(vmem_limit_bytes=4 << 20),
        name="join",
    )(*parts, *after)


def prepare_kernel(place_ref, damp_ref, *refs):
    pieces, rows = refs[:NZ], refs[-1]
    left_ref, right_ref, in_ref, back_ref, scale_ref = refs[-6:-1]
    y, z, c = coordinates(place_ref[0])
    for dz in range(NZ):
        for dy in range(NY):
            for dc in range(NC):
                owner = ((y - dy) & 3) * 8 + ((z - dz) & 3) * 2 + (c ^ dc)
                k = dy * NC + dc
                piece = pieces[dz][8 * k : 8 * k + 8, :]
                rows[pl.ds(pl.multiple_of(owner * 8, 8), 8), :] = piece
    table = rows[...]
    high, low = split2(table)
    lowest = (table - high.astype(F32) - low.astype(F32)).astype(BF16)

    def iota(shape, axis):
        return lax.broadcasted_iota(jnp.int32, shape, axis)

    def pick(condition):
        return condition.astype(F32).astype(BF16)

    r, k = iota((IN, 256), 0), iota((IN, 256), 1)
    pick_in = pick(k == (r // 4) * 8 + r % 4)
    basis, rest = mm(pick_in, high), mm(pick_in, low)
    in_ref[...] = jnp.concatenate([basis, rest], axis=0).astype(BF16)
    turned, turned_rest = basis.T, rest.T
    back_ref[...] = jnp.concatenate(
        [
            jnp.concatenate([turned, turned_rest], axis=1),
            jnp.concatenate([turned, jnp.zeros_like(turned)], axis=1),
        ],
        axis=0,
    ).astype(BF16)
    r, k = iota((256, 256), 0), iota((256, 256), 1)
    pick_eig = pick(k == (r // 8) * 8 + 4)
    eig = mm(pick_eig, high) + (mm(pick_eig, low) + mm(pick_eig, lowest))
    scale_ref[...] = 1.0 / (eig + damp_ref[0])
    pick_out = pick(k == (r // 8) * 8 + 5)
    spread = pick(iota((IN, 256), 0) == iota((IN, 256), 1) // 8)
    same = (r % 8 == k % 8).astype(F32)
    for term, part in enumerate((high, low)):
        whole = mm(mm(pick_out, part).astype(BF16), spread) * same
        right_ref[256 * term : 256 * (term + 1), :] = whole.astype(BF16)
        left_ref[256 * term : 256 * (term + 1), :] = whole.T.astype(BF16)


def prepare(place, damping, pieces, after):
    shape = jax.ShapeDtypeStruct
    return pl.pallas_call(
        prepare_kernel,
        out_shape=(
            shape((512, 256), BF16),
            shape((512, 256), BF16),
            shape((2 * IN, IN), BF16),
            shape((2 * IN, 2 * IN), BF16),
            shape((256, IN), F32),
        ),
        in_specs=[SMEM, SMEM] + [VMEM] * NZ + [ANY] * len(after),
        out_specs=(VMEM,) * 5,
        scratch_shapes=[pltpu.VMEM((256, 128), F32)],
        compiler_params=pltpu.CompilerParams(vmem_limit_bytes=16 << 20),
        cost_estimate=pl.CostEstimate(flops=200_000_000, bytes_accessed=1 << 20, transcendentals=0),
        name="prepare",
    )(place, damping, *pieces, *after)


def mix(matrix, x):
    high, low = split2(x)
    both = mm(matrix, high)
    return both[:256] + (both[256:] + mm(matrix[:256], low))


def rotate_chunk(x, left, right, basis, back, scale):
    count = 2 * len(x)
    tall = jnp.concatenate(
        [piece[:, IN * i : IN * (i + 1)] for piece in x for i in range(OUT)], axis=0
    )
    half = mm(jnp.concatenate([tall, tall], axis=1), basis)
    half = half.reshape(count // 2, OUT, 2, 8, IN)
    side = jnp.concatenate(
        [half[g // 2, :, g % 2].reshape(OUT * 8, IN) for g in range(count)], axis=1
    )
    rotated = mix(left, side)
    scaled = jnp.concatenate(
        [rotated[:, IN * g : IN * (g + 1)] * scale for g in range(count)], axis=0
    )
    restored = mm(jnp.concatenate(split2(scaled), axis=1), back)
    restored = restored[:, :IN] + restored[:, IN:]
    side = jnp.concatenate([restored[256 * g : 256 * (g + 1)] for g in range(count)], axis=1)
    return mix(right, side)


def rotate_kernel(most, count, left_ref, right_ref, in_ref, back_ref, scale_ref, *refs):
    blocks, out_ref = refs[:count], refs[-1]
    pieces = [(b, at) for b in blocks for at in range(0, b.shape[0], 16)]
    step = -(-len(pieces) // -(-len(pieces) // most))
    for first in range(0, len(pieces), step):
        chunk = pieces[first : first + step]
        done = rotate_chunk(
            [b[at : at + 16, :] for b, at in chunk],
            left_ref[...],
            right_ref[...],
            in_ref[...],
            back_ref[...],
            scale_ref[...],
        )
        for p in range(len(chunk)):
            to = 16 * (first + p)
            for i in range(OUT):
                rows = done[8 * i : 8 * i + 8, 2 * IN * p : 2 * IN * (p + 1)]
                rows = jnp.concatenate([rows[:, :IN], rows[:, IN:]], axis=0)
                out_ref[to : to + 16, IN * i : IN * (i + 1)] = rows.astype(BF16)


def rotate(tables, blocks, after):
    rows = sum(b.shape[0] for b in blocks)
    width = blocks[0].shape[1]
    return pl.pallas_call(
        functools.partial(rotate_kernel, CHUNK, len(blocks)),
        out_shape=jax.ShapeDtypeStruct((rows, width), BF16),
        in_specs=[VMEM] * (5 + len(blocks)) + [ANY] * len(after),
        out_specs=VMEM,
        compiler_params=pltpu.CompilerParams(vmem_limit_bytes=32 << 20),
        cost_estimate=pl.CostEstimate(flops=0, bytes_accessed=0, transcendentals=0),
        name="rotate",
    )(*tables, *blocks, *after)


def scores_of(conditioned, documents):
    return lax.dot_general(
        conditioned, documents, (((1,), (1,)), ((), ())), preferred_element_type=F32
    ).astype(BF16)


def arrange_kernel(offsets, place_ref, *refs):
    parts, out_ref = refs[: 2 * len(offsets)], refs[-1]
    y, z, c = coordinates(place_ref[0])
    layer = place_ref[1]
    for k, part in enumerate(parts):
        kind = c ^ (k % 2)
        for at, (dy, dz) in enumerate(offsets[k // 2]):
            from_z = (z - dz) & 3
            to = ((y - dy) & 3) * 2 + (from_z >> 1)
            turn = ((to ^ layer) & 4) + ((to - layer) & 3)
            out_ref[turn * 4 + (from_z & 1) * 2 + kind] = part[ROWS * at : ROWS * (at + 1), :]


def arrange(place, offsets, parts, after):
    count = sum(p.shape[0] for p in parts) // ROWS
    columns = parts[0].shape[1]
    return pl.pallas_call(
        functools.partial(arrange_kernel, offsets),
        out_shape=jax.ShapeDtypeStruct((count, ROWS, columns), BF16),
        in_specs=[SMEM] + [VMEM] * len(parts) + [ANY] * len(after),
        out_specs=VMEM,
        compiler_params=pltpu.CompilerParams(vmem_limit_bytes=16 << 20),
        cost_estimate=pl.CostEstimate(
            flops=0, bytes_accessed=count * ROWS * columns * 4, transcendentals=0
        ),
        name="arrange",
    )(place, *parts, *after)


def finish_kernel(*refs):
    total = refs[0][...].astype(F32)
    for part in refs[1:-1]:
        total += part[...].astype(F32)
    refs[-1][...] = total


def finish(parts):
    return pl.pallas_call(
        finish_kernel,
        out_shape=jax.ShapeDtypeStruct(parts[0].shape, F32),
        in_specs=[VMEM] * len(parts),
        out_specs=VMEM,
        compiler_params=pltpu.CompilerParams(vmem_limit_bytes=8 << 20),
        name="finish",
    )(*parts)


def spread_over_layers(ready):
    ready = ready.reshape(NL * NX, 4 * ROWS, ready.shape[-1])
    parts = [ready[0]]
    for dl, dx in ((1, 2), (0, 2), (1, 1), (1, 3), (1, 0), (0, 1), (0, 3)):
        parts.append(lax.ppermute(ready[dl * NX + dx], "layer", layer_shift(dl, dx)))
    return parts


def halves_kernel(behind_ref, ahead_ref, *refs):
    first_ref, second_ref = refs[-2:]
    rows = first_ref.shape[0]
    first_ref[...] = behind_ref[:rows, :]
    second_ref[...] = ahead_ref[rows:, :]


def halves(behind, ahead, after):
    rows, columns = behind.shape
    return pl.pallas_call(
        halves_kernel,
        out_shape=(jax.ShapeDtypeStruct((rows // 2, columns), behind.dtype),) * 2,
        in_specs=[VMEM, VMEM] + [ANY] * len(after),
        out_specs=(VMEM, VMEM),
        compiler_params=pltpu.CompilerParams(vmem_limit_bytes=4 << 20),
        name="halves",
    )(behind, ahead, *after)


def both_ways(own, axis):
    return send(own, **{axis: 1}), send(own, **{axis: -1})


def body(query_grads, doc_grads, out_basis, in_basis, eigenvalues, damping):
    place = jnp.stack([lax.axis_index("example"), lax.axis_index("layer")])

    own, docs = query_grads[0], doc_grads[0]
    docs_there = send(docs, dc=1)

    near = both_ways(own, "dz")
    row = pack(in_basis[0], eigenvalues[0], out_basis[0])
    pair = join([row, send(row, dc=1)], [])
    column = [send(pair, dy=d) for d in range(1, NY)]
    plane = join([pair] + column, [docs_there])
    pieces = [plane] + [send(plane, dz=d) for d in range(1, NZ)]
    tables = prepare(place, damping, pieces, [])

    side = join([own, *near], pieces[1:2])
    side_y = both_ways(side, "dy")

    cut = halves(*near, pieces[1:3])
    far = send(cut[0], dz=1), send(cut[1], dz=-1)
    other = join(far, [])
    other_y = both_ways(other, "dy")

    first = rotate(tables, (own, *near), [])
    low = join([side_y[1]], [first], [(ROWS, 3 * ROWS)])
    high = join([side_y[0], other_y[0]], [first], [(0, ROWS), (0, ROWS)])
    side_far = send(high, dy=1), send(low, dy=-1)

    offsets = [
        [(0, 0), (0, 1), (0, -1)],
        [(1, 0), (1, 1), (1, -1), (-1, 0), (-1, 1), (-1, -1), (0, 2)],
        [(1, 2), (-1, 2)],
        [(2, 0), (2, 2), (2, 1), (2, -1)],
    ]

    docs_other = held(docs_there, [first, other])

    def scored(conditioned):
        theirs = send(scores_of(conditioned, docs_other), dc=1)
        return [scores_of(conditioned, docs), theirs]

    parts = scored(first)
    parts += scored(rotate(tables, (*side_y, other), [low, parts[0]]))
    parts += scored(rotate(tables, other_y, [high, parts[2]]))
    parts += scored(rotate(tables, side_far, parts[4:5]))
    return finish(spread_over_layers(arrange(place, offsets, parts, [])))


def solution(mesh):
    placed = P("layer", "example", None)
    return jax.shard_map(
        body,
        mesh=mesh,
        in_specs=(placed,) * 5 + (P("layer"),),
        out_specs=P("layer", "example"),
        check_vma=False,
    )
```

```python
import functools
import jax
import jax.numpy as jnp
from jax import lax
from jax.experimental import pallas as pl
from jax.experimental.pallas import tpu as pltpu
from jax.sharding import PartitionSpec as P

NY, NZ, NC = 4, 4, 2
NL, NX = 2, 4
ROWS = 32
CHUNK = 8
OUT, IN = 32, 128
F32, BF16 = jnp.float32, jnp.bfloat16
VMEM = pl.BlockSpec(memory_space=pltpu.VMEM)
SMEM = pl.BlockSpec(memory_space=pltpu.SMEM)
ANY = pl.BlockSpec(memory_space=pl.ANY)
HBM = pl.BlockSpec(memory_space=pltpu.HBM)


def example_shift(dy, dz, dc):
    def place(y, z, c):
        return (y % NY) * NZ * NC + (z % NZ) * NC + c % NC

    return [
        (place(y, z, c), place(y + dy, z + dz, c + dc))
        for y in range(NY)
        for z in range(NZ)
        for c in range(NC)
    ]


def layer_shift(dl, dx):
    return [
        (a * NX + x, ((a + dl) % NL) * NX + (x + dx) % NX) for a in range(NL) for x in range(NX)
    ]


def send(x, dy=0, dz=0, dc=0):
    return lax.ppermute(x, "example", example_shift(dy, dz, dc))


def split2(x):
    high = x.astype(BF16)
    return high, (x - high.astype(F32)).astype(BF16)


def mm(a, b, contract=((1,), (0,))):
    return lax.dot_general(a, b, (contract, ((), ())), preferred_element_type=F32)


def coordinates(example):
    return example >> 3, (example >> 1) & 3, example & 1


def held_kernel(x_ref, *refs):
    pltpu.sync_copy(x_ref, refs[-1])


def held(x, after=()):
    return pl.pallas_call(
        held_kernel,
        out_shape=jax.ShapeDtypeStruct(x.shape, x.dtype),
        in_specs=[HBM] + [ANY] * len(after),
        out_specs=VMEM,
        compiler_params=pltpu.CompilerParams(vmem_limit_bytes=16 << 20),
        cost_estimate=pl.CostEstimate(flops=0, bytes_accessed=2 * x.nbytes, transcendentals=0),
        name="held",
    )(x, *after)


def pack_kernel(in_ref, eig_ref, basis_ref, out_ref, in_rows, eig_rows, basis_rows, sems):
    copies = [
        pltpu.make_async_copy(source, target, sems.at[k])
        for k, (source, target) in enumerate(
            ((in_ref, in_rows), (eig_ref, eig_rows), (basis_ref, basis_rows))
        )
    ]
    for copy in copies:
        copy.start()
    out_ref[...] = jnp.zeros_like(out_ref)
    for copy in copies:
        copy.wait()
    out_ref[0:4, :] = in_rows[...]
    out_ref[4:5, :] = eig_rows[...]
    out_ref[5:6, 0:OUT] = basis_rows[...]


def pack(*parts):
    return pl.pallas_call(
        pack_kernel,
        out_shape=jax.ShapeDtypeStruct((8, IN), F32),
        in_specs=[HBM] * 3,
        out_specs=VMEM,
        scratch_shapes=[pltpu.VMEM(p.shape, p.dtype) for p in parts]
        + [pltpu.SemaphoreType.DMA((3,))],
        compiler_params=pltpu.CompilerParams(vmem_limit_bytes=1 << 20),
        name="pack",
    )(*parts)


def join_kernel(ranges, *refs):
    out_ref, at = refs[-1], 0
    for part, (low, high) in zip(refs, ranges):
        out_ref[at : at + high - low, :] = part[low:high, :]
        at += high - low


def join(parts, after, ranges=None):
    ranges = ranges or [(0, p.shape[0]) for p in parts]
    rows = sum(high - low for low, high in ranges)
    columns, dtype = parts[0].shape[1], parts[0].dtype
    return pl.pallas_call(
        functools.partial(join_kernel, ranges),
        out_shape=jax.ShapeDtypeStruct((rows, columns), dtype),
        in_specs=[VMEM] * len(parts) + [ANY] * len(after),
        out_specs=VMEM,
        compiler_params=pltpu.CompilerParams(vmem_limit_bytes=8 << 20),
        name="join",
    )(*parts, *after)


def prepare_kernel(place_ref, damp_ref, *refs):
    pieces, rows = refs[:NZ], refs[-1]
    left_ref, right_ref, in_ref, back_ref, scale_ref = refs[-6:-1]
    y, z, c = coordinates(place_ref[0])
    for dz in range(NZ):
        for dy in range(NY):
            for dc in range(NC):
                owner = ((y - dy) & 3) * 8 + ((z - dz) & 3) * 2 + (c ^ dc)
                k = dy * NC + dc
                piece = pieces[dz][8 * k : 8 * k + 8, :]
                rows[pl.ds(pl.multiple_of(owner * 8, 8), 8), :] = piece
    table = rows[...]
    high, low = split2(table)
    lowest = (table - high.astype(F32) - low.astype(F32)).astype(BF16)

    def iota(shape, axis):
        return lax.broadcasted_iota(jnp.int32, shape, axis)

    def pick(condition):
        return condition.astype(F32).astype(BF16)

    r, k = iota((IN, 256), 0), iota((IN, 256), 1)
    pick_in = pick(k == (r // 4) * 8 + r % 4)
    basis, rest = mm(pick_in, high), mm(pick_in, low)
    in_ref[...] = jnp.concatenate([basis, rest], axis=0).astype(BF16)
    turned, turned_rest = basis.T, rest.T
    back_ref[...] = jnp.concatenate(
        [
            jnp.concatenate([turned, turned_rest], axis=1),
            jnp.concatenate([turned, jnp.zeros_like(turned)], axis=1),
        ],
        axis=0,
    ).astype(BF16)
    r, k = iota((256, 256), 0), iota((256, 256), 1)
    pick_eig = pick(k == (r // 8) * 8 + 4)
    eig = mm(pick_eig, high) + (mm(pick_eig, low) + mm(pick_eig, lowest))
    scale_ref[...] = 1.0 / (eig + damp_ref[0])
    pick_out = pick(k == (r // 8) * 8 + 5)
    spread = pick(iota((IN, 256), 0) == iota((IN, 256), 1) // 8)
    same = (r % 8 == k % 8).astype(F32)
    for term, part in enumerate((high, low)):
        whole = mm(mm(pick_out, part).astype(BF16), spread) * same
        right_ref[256 * term : 256 * (term + 1), :] = whole.astype(BF16)
        left_ref[256 * term : 256 * (term + 1), :] = whole.T.astype(BF16)


def prepare(place, damping, pieces, after):
    shape = jax.ShapeDtypeStruct
    return pl.pallas_call(
        prepare_kernel,
        out_shape=(
            shape((512, 256), BF16),
            shape((512, 256), BF16),
            shape((2 * IN, IN), BF16),
            shape((2 * IN, 2 * IN), BF16),
            shape((256, IN), F32),
        ),
        in_specs=[SMEM, SMEM] + [VMEM] * NZ + [ANY] * len(after),
        out_specs=(VMEM,) * 5,
        scratch_shapes=[pltpu.VMEM((256, 128), F32)],
        compiler_params=pltpu.CompilerParams(vmem_limit_bytes=16 << 20),
        cost_estimate=pl.CostEstimate(flops=200_000_000, bytes_accessed=1 << 20, transcendentals=0),
        name="prepare",
    )(place, damping, *pieces, *after)


def mix(matrix, x):
    high, low = split2(x)
    both = mm(matrix, high)
    return both[:256] + (both[256:] + mm(matrix[:256], low))


def rotate_chunk(x, left, right, basis, back, scale):
    count = 2 * len(x)
    tall = jnp.concatenate(
        [piece[:, IN * i : IN * (i + 1)] for piece in x for i in range(OUT)], axis=0
    )
    half = mm(jnp.concatenate([tall, tall], axis=1), basis)
    half = half.reshape(count // 2, OUT, 2, 8, IN)
    side = jnp.concatenate(
        [half[g // 2, :, g % 2].reshape(OUT * 8, IN) for g in range(count)], axis=1
    )
    rotated = mix(left, side)
    scaled = jnp.concatenate(
        [rotated[:, IN * g : IN * (g + 1)] * scale for g in range(count)], axis=0
    )
    restored = mm(jnp.concatenate(split2(scaled), axis=1), back)
    restored = restored[:, :IN] + restored[:, IN:]
    side = jnp.concatenate([restored[256 * g : 256 * (g + 1)] for g in range(count)], axis=1)
    return mix(right, side)


def rotate_kernel(most, count, left_ref, right_ref, in_ref, back_ref, scale_ref, *refs):
    blocks, out_ref = refs[:count], refs[-1]
    pieces = [(b, at) for b in blocks for at in range(0, b.shape[0], 16)]
    step = -(-len(pieces) // -(-len(pieces) // most))
    for first in range(0, len(pieces), step):
        chunk = pieces[first : first + step]
        done = rotate_chunk(
            [b[at : at + 16, :] for b, at in chunk],
            left_ref[...],
            right_ref[...],
            in_ref[...],
            back_ref[...],
            scale_ref[...],
        )
        for p in range(len(chunk)):
            to = 16 * (first + p)
            for i in range(OUT):
                rows = done[8 * i : 8 * i + 8, 2 * IN * p : 2 * IN * (p + 1)]
                rows = jnp.concatenate([rows[:, :IN], rows[:, IN:]], axis=0)
                out_ref[to : to + 16, IN * i : IN * (i + 1)] = rows.astype(BF16)


def rotate(tables, blocks, after, flops=0):
    rows = sum(b.shape[0] for b in blocks)
    width = blocks[0].shape[1]
    return pl.pallas_call(
        functools.partial(rotate_kernel, CHUNK, len(blocks)),
        out_shape=jax.ShapeDtypeStruct((rows, width), BF16),
        in_specs=[VMEM] * (5 + len(blocks)) + [ANY] * len(after),
        out_specs=VMEM,
        compiler_params=pltpu.CompilerParams(vmem_limit_bytes=32 << 20),
        cost_estimate=pl.CostEstimate(flops=flops, bytes_accessed=0, transcendentals=0),
        name="rotate",
    )(*tables, *blocks, *after)


def scores_of(conditioned, documents):
    return lax.dot_general(
        conditioned, documents, (((1,), (1,)), ((), ())), preferred_element_type=F32
    ).astype(BF16)


def arrange_kernel(offsets, place_ref, *refs):
    parts, out_ref = refs[: 2 * len(offsets)], refs[-1]
    y, z, c = coordinates(place_ref[0])
    layer = place_ref[1]
    for k, part in enumerate(parts):
        kind = c ^ (k % 2)
        for at, (dy, dz) in enumerate(offsets[k // 2]):
            from_z = (z - dz) & 3
            to = ((y - dy) & 3) * 2 + (from_z >> 1)
            turn = ((to ^ layer) & 4) + ((to - layer) & 3)
            out_ref[turn * 4 + (from_z & 1) * 2 + kind] = part[ROWS * at : ROWS * (at + 1), :]


def arrange(place, offsets, parts, after):
    count = sum(p.shape[0] for p in parts) // ROWS
    columns = parts[0].shape[1]
    return pl.pallas_call(
        functools.partial(arrange_kernel, offsets),
        out_shape=jax.ShapeDtypeStruct((count, ROWS, columns), BF16),
        in_specs=[SMEM] + [VMEM] * len(parts) + [ANY] * len(after),
        out_specs=VMEM,
        compiler_params=pltpu.CompilerParams(vmem_limit_bytes=16 << 20),
        cost_estimate=pl.CostEstimate(
            flops=0, bytes_accessed=count * ROWS * columns * 4, transcendentals=0
        ),
        name="arrange",
    )(place, *parts, *after)


def finish_kernel(*refs):
    total = refs[0][...].astype(F32)
    for part in refs[1:-1]:
        total += part[...].astype(F32)
    refs[-1][...] = total


def finish(parts):
    return pl.pallas_call(
        finish_kernel,
        out_shape=jax.ShapeDtypeStruct(parts[0].shape, F32),
        in_specs=[VMEM] * len(parts),
        out_specs=VMEM,
        compiler_params=pltpu.CompilerParams(vmem_limit_bytes=8 << 20),
        name="finish",
    )(*parts)


def spread_over_layers(ready):
    ready = ready.reshape(NL * NX, 4 * ROWS, ready.shape[-1])
    parts = [ready[0]]
    for dl, dx in ((1, 2), (0, 2), (1, 1), (1, 3), (1, 0), (0, 1), (0, 3)):
        parts.append(lax.ppermute(ready[dl * NX + dx], "layer", layer_shift(dl, dx)))
    return parts


def halves_kernel(behind_ref, ahead_ref, *refs):
    first_ref, second_ref = refs[-2:]
    rows = first_ref.shape[0]
    first_ref[...] = behind_ref[:rows, :]
    second_ref[...] = ahead_ref[rows:, :]


def halves(behind, ahead, after):
    rows, columns = behind.shape
    return pl.pallas_call(
        halves_kernel,
        out_shape=(jax.ShapeDtypeStruct((rows // 2, columns), behind.dtype),) * 2,
        in_specs=[VMEM, VMEM] + [ANY] * len(after),
        out_specs=(VMEM, VMEM),
        compiler_params=pltpu.CompilerParams(vmem_limit_bytes=4 << 20),
        name="halves",
    )(behind, ahead, *after)


def both_ways(own, axis):
    return send(own, **{axis: 1}), send(own, **{axis: -1})


def body(query_grads, doc_grads, out_basis, in_basis, eigenvalues, damping):
    place = jnp.stack([lax.axis_index("example"), lax.axis_index("layer")])

    own, docs = query_grads[0], doc_grads[0]
    docs_there = send(docs, dc=1)

    near = both_ways(own, "dz")
    row = pack(in_basis[0], eigenvalues[0], out_basis[0])
    pair = join([row, send(row, dc=1)], [])
    column = [send(pair, dy=d) for d in range(1, NY)]
    plane = join([pair] + column, [docs_there])
    pieces = [plane] + [send(plane, dz=d) for d in range(1, NZ)]
    tables = prepare(place, damping, pieces, [])

    cut = halves(*near, pieces[1:3])
    far = send(cut[0], dz=1), send(cut[1], dz=-1)

    side = rotate(tables, (own, *near), [cut[0]])
    side_y = both_ways(side, "dy")
    other = rotate(tables, far, [side], 20_000_000_000)
    other_y = both_ways(other, "dy")

    low = join([side_y[1]], [], [(ROWS, 3 * ROWS)])
    high = join([side_y[0], other_y[0]], [], [(0, ROWS), (0, ROWS)])
    side_far = send(high, dy=1), send(low, dy=-1)

    docs_other = held(docs_there, [other])

    offsets = [
        [(0, 0), (0, 1), (0, -1), (0, 2)],
        [(1, 0), (1, 1), (1, -1), (-1, 0), (-1, 1), (-1, -1), (1, 2), (-1, 2)],
        [(2, 0), (2, 2), (2, 1), (2, -1)],
    ]
    parts = []
    for blocks, after in (((side, other), [docs_other]), ((*side_y, *other_y), [high, low]), (side_far, [])):
        conditioned = join(blocks, after + parts[-2:-1])
        theirs = send(scores_of(conditioned, docs_other), dc=1)
        parts += [scores_of(conditioned, docs), theirs]
    return finish(spread_over_layers(arrange(place, offsets, parts, [])))


def solution(mesh):
    placed = P("layer", "example", None)
    return jax.shard_map(
        body,
        mesh=mesh,
        in_specs=(placed,) * 5 + (P("layer"),),
        out_specs=P("layer", "example"),
        check_vma=False,
    )
```

```python
import functools
import jax
import jax.numpy as jnp
from jax import lax
from jax.experimental import pallas as pl
from jax.experimental.pallas import tpu as pltpu
from jax.sharding import PartitionSpec as P

NY, NZ, NC = 4, 4, 2
NL, NX = 2, 4
ROWS = 32
CHUNK = 8
OUT, IN = 32, 128
F32, BF16 = jnp.float32, jnp.bfloat16
VMEM = pl.BlockSpec(memory_space=pltpu.VMEM)
SMEM = pl.BlockSpec(memory_space=pltpu.SMEM)
ANY = pl.BlockSpec(memory_space=pl.ANY)
HBM = pl.BlockSpec(memory_space=pltpu.HBM)


def example_shift(dy, dz, dc):
    def place(y, z, c):
        return (y % NY) * NZ * NC + (z % NZ) * NC + c % NC

    return [
        (place(y, z, c), place(y + dy, z + dz, c + dc))
        for y in range(NY)
        for z in range(NZ)
        for c in range(NC)
    ]


def layer_shift(dl, dx):
    return [
        (a * NX + x, ((a + dl) % NL) * NX + (x + dx) % NX) for a in range(NL) for x in range(NX)
    ]


def send(x, dy=0, dz=0, dc=0):
    return lax.ppermute(x, "example", example_shift(dy, dz, dc))


def split2(x):
    high = x.astype(BF16)
    return high, (x - high.astype(F32)).astype(BF16)


def mm(a, b, contract=((1,), (0,))):
    return lax.dot_general(a, b, (contract, ((), ())), preferred_element_type=F32)


def coordinates(example):
    return example >> 3, (example >> 1) & 3, example & 1


def held_kernel(x_ref, *refs):
    pltpu.sync_copy(x_ref, refs[-1])


def held(x, after=()):
    return pl.pallas_call(
        held_kernel,
        out_shape=jax.ShapeDtypeStruct(x.shape, x.dtype),
        in_specs=[HBM] + [ANY] * len(after),
        out_specs=VMEM,
        compiler_params=pltpu.CompilerParams(vmem_limit_bytes=16 << 20),
        cost_estimate=pl.CostEstimate(flops=0, bytes_accessed=2 * x.nbytes, transcendentals=0),
        name="held",
    )(x, *after)


def pack_kernel(in_ref, eig_ref, basis_ref, out_ref, in_rows, eig_rows, basis_rows, sems):
    copies = [
        pltpu.make_async_copy(source, target, sems.at[k])
        for k, (source, target) in enumerate(
            ((in_ref, in_rows), (eig_ref, eig_rows), (basis_ref, basis_rows))
        )
    ]
    for copy in copies:
        copy.start()
    out_ref[...] = jnp.zeros_like(out_ref)
    for copy in copies:
        copy.wait()
    out_ref[0:4, :] = in_rows[...]
    out_ref[4:5, :] = eig_rows[...]
    out_ref[5:6, 0:OUT] = basis_rows[...]


def pack(*parts):
    return pl.pallas_call(
        pack_kernel,
        out_shape=jax.ShapeDtypeStruct((8, IN), F32),
        in_specs=[HBM] * 3,
        out_specs=VMEM,
        scratch_shapes=[pltpu.VMEM(p.shape, p.dtype) for p in parts]
        + [pltpu.SemaphoreType.DMA((3,))],
        compiler_params=pltpu.CompilerParams(vmem_limit_bytes=1 << 20),
        name="pack",
    )(*parts)


def join_kernel(ranges, *refs):
    out_ref, at = refs[-1], 0
    for part, (low, high) in zip(refs, ranges):
        out_ref[at : at + high - low, :] = part[low:high, :]
        at += high - low


def join(parts, after, ranges=None):
    ranges = ranges or [(0, p.shape[0]) for p in parts]
    rows = sum(high - low for low, high in ranges)
    columns, dtype = parts[0].shape[1], parts[0].dtype
    return pl.pallas_call(
        functools.partial(join_kernel, ranges),
        out_shape=jax.ShapeDtypeStruct((rows, columns), dtype),
        in_specs=[VMEM] * len(parts) + [ANY] * len(after),
        out_specs=VMEM,
        compiler_params=pltpu.CompilerParams(vmem_limit_bytes=8 << 20),
        name="join",
    )(*parts, *after)


def prepare_kernel(place_ref, damp_ref, *refs):
    pieces, rows = refs[:NZ], refs[-1]
    left_ref, right_ref, in_ref, back_ref, scale_ref = refs[-6:-1]
    y, z, c = coordinates(place_ref[0])
    for dz in range(NZ):
        for dy in range(NY):
            for dc in range(NC):
                owner = ((y - dy) & 3) * 8 + ((z - dz) & 3) * 2 + (c ^ dc)
                k = dy * NC + dc
                piece = pieces[dz][8 * k : 8 * k + 8, :]
                rows[pl.ds(pl.multiple_of(owner * 8, 8), 8), :] = piece
    table = rows[...]
    high, low = split2(table)
    lowest = (table - high.astype(F32) - low.astype(F32)).astype(BF16)

    def iota(shape, axis):
        return lax.broadcasted_iota(jnp.int32, shape, axis)

    def pick(condition):
        return condition.astype(F32).astype(BF16)

    r, k = iota((IN, 256), 0), iota((IN, 256), 1)
    pick_in = pick(k == (r // 4) * 8 + r % 4)
    basis, rest = mm(pick_in, high), mm(pick_in, low)
    in_ref[...] = jnp.concatenate([basis, rest], axis=0).astype(BF16)
    turned, turned_rest = basis.T, rest.T
    back_ref[...] = jnp.concatenate(
        [
            jnp.concatenate([turned, turned_rest], axis=1),
            jnp.concatenate([turned, jnp.zeros_like(turned)], axis=1),
        ],
        axis=0,
    ).astype(BF16)
    r, k = iota((256, 256), 0), iota((256, 256), 1)
    pick_eig = pick(k == (r // 8) * 8 + 4)
    eig = mm(pick_eig, high) + (mm(pick_eig, low) + mm(pick_eig, lowest))
    scale_ref[...] = 1.0 / (eig + damp_ref[0])
    pick_out = pick(k == (r // 8) * 8 + 5)
    spread = pick(iota((IN, 256), 0) == iota((IN, 256), 1) // 8)
    same = (r % 8 == k % 8).astype(F32)
    for term, part in enumerate((high, low)):
        whole = mm(mm(pick_out, part).astype(BF16), spread) * same
        right_ref[256 * term : 256 * (term + 1), :] = whole.astype(BF16)
        left_ref[256 * term : 256 * (term + 1), :] = whole.T.astype(BF16)


def prepare(place, damping, pieces, after):
    shape = jax.ShapeDtypeStruct
    return pl.pallas_call(
        prepare_kernel,
        out_shape=(
            shape((512, 256), BF16),
            shape((512, 256), BF16),
            shape((2 * IN, IN), BF16),
            shape((2 * IN, 2 * IN), BF16),
            shape((256, IN), F32),
        ),
        in_specs=[SMEM, SMEM] + [VMEM] * NZ + [ANY] * len(after),
        out_specs=(VMEM,) * 5,
        scratch_shapes=[pltpu.VMEM((256, 128), F32)],
        compiler_params=pltpu.CompilerParams(vmem_limit_bytes=16 << 20),
        cost_estimate=pl.CostEstimate(flops=200_000_000, bytes_accessed=1 << 20, transcendentals=0),
        name="prepare",
    )(place, damping, *pieces, *after)


def mix(matrix, x):
    high, low = split2(x)
    both = mm(matrix, high)
    return both[:256] + (both[256:] + mm(matrix[:256], low))


def rotate_chunk(x, left, right, basis, back, scale):
    count = 2 * len(x)
    tall = jnp.concatenate(
        [piece[:, IN * i : IN * (i + 1)] for piece in x for i in range(OUT)], axis=0
    )
    half = mm(jnp.concatenate([tall, tall], axis=1), basis)
    half = half.reshape(count // 2, OUT, 2, 8, IN)
    side = jnp.concatenate(
        [half[g // 2, :, g % 2].reshape(OUT * 8, IN) for g in range(count)], axis=1
    )
    rotated = mix(left, side)
    scaled = jnp.concatenate(
        [rotated[:, IN * g : IN * (g + 1)] * scale for g in range(count)], axis=0
    )
    restored = mm(jnp.concatenate(split2(scaled), axis=1), back)
    restored = restored[:, :IN] + restored[:, IN:]
    side = jnp.concatenate([restored[256 * g : 256 * (g + 1)] for g in range(count)], axis=1)
    return mix(right, side)


def rotate_kernel(most, count, left_ref, right_ref, in_ref, back_ref, scale_ref, *refs):
    blocks, out_ref = refs[:count], refs[-1]
    pieces = [(b, at) for b in blocks for at in range(0, b.shape[0], 16)]
    step = -(-len(pieces) // -(-len(pieces) // most))
    for first in range(0, len(pieces), step):
        chunk = pieces[first : first + step]
        done = rotate_chunk(
            [b[at : at + 16, :] for b, at in chunk],
            left_ref[...],
            right_ref[...],
            in_ref[...],
            back_ref[...],
            scale_ref[...],
        )
        for p in range(len(chunk)):
            to = 16 * (first + p)
            for i in range(OUT):
                rows = done[8 * i : 8 * i + 8, 2 * IN * p : 2 * IN * (p + 1)]
                rows = jnp.concatenate([rows[:, :IN], rows[:, IN:]], axis=0)
                out_ref[to : to + 16, IN * i : IN * (i + 1)] = rows.astype(BF16)


def rotate(tables, blocks, after, flops=0):
    rows = sum(b.shape[0] for b in blocks)
    width = blocks[0].shape[1]
    return pl.pallas_call(
        functools.partial(rotate_kernel, CHUNK, len(blocks)),
        out_shape=jax.ShapeDtypeStruct((rows, width), BF16),
        in_specs=[VMEM] * (5 + len(blocks)) + [ANY] * len(after),
        out_specs=VMEM,
        compiler_params=pltpu.CompilerParams(vmem_limit_bytes=32 << 20),
        cost_estimate=pl.CostEstimate(flops=flops, bytes_accessed=0, transcendentals=0),
        name="rotate",
    )(*tables, *blocks, *after)


def scores_of(conditioned, documents):
    return lax.dot_general(
        conditioned, documents, (((1,), (1,)), ((), ())), preferred_element_type=F32
    ).astype(BF16)


def arrange_kernel(offsets, place_ref, *refs):
    parts, out_ref = refs[: 2 * len(offsets)], refs[-1]
    y, z, c = coordinates(place_ref[0])
    layer = place_ref[1]
    for k, part in enumerate(parts):
        kind = c ^ (k % 2)
        for at, (dy, dz) in enumerate(offsets[k // 2]):
            from_z = (z - dz) & 3
            to = ((y - dy) & 3) * 2 + (from_z >> 1)
            turn = ((to ^ layer) & 4) + ((to - layer) & 3)
            out_ref[turn * 4 + (from_z & 1) * 2 + kind] = part[ROWS * at : ROWS * (at + 1), :]


def arrange(place, offsets, parts, after):
    count = sum(p.shape[0] for p in parts) // ROWS
    columns = parts[0].shape[1]
    return pl.pallas_call(
        functools.partial(arrange_kernel, offsets),
        out_shape=jax.ShapeDtypeStruct((count, ROWS, columns), BF16),
        in_specs=[SMEM] + [VMEM] * len(parts) + [ANY] * len(after),
        out_specs=VMEM,
        compiler_params=pltpu.CompilerParams(vmem_limit_bytes=16 << 20),
        cost_estimate=pl.CostEstimate(
            flops=0, bytes_accessed=count * ROWS * columns * 4, transcendentals=0
        ),
        name="arrange",
    )(place, *parts, *after)


def finish_kernel(*refs):
    total = refs[0][...].astype(F32)
    for part in refs[1:-1]:
        total += part[...].astype(F32)
    refs[-1][...] = total


def finish(parts):
    return pl.pallas_call(
        finish_kernel,
        out_shape=jax.ShapeDtypeStruct(parts[0].shape, F32),
        in_specs=[VMEM] * len(parts),
        out_specs=VMEM,
        compiler_params=pltpu.CompilerParams(vmem_limit_bytes=8 << 20),
        name="finish",
    )(*parts)


def spread_over_layers(ready):
    ready = ready.reshape(NL * NX, 4 * ROWS, ready.shape[-1])
    parts = [ready[0]]
    for dl, dx in ((1, 0), (0, 1), (1, 2), (0, 2), (1, 1), (1, 3), (0, 3)):
        parts.append(lax.ppermute(ready[dl * NX + dx], "layer", layer_shift(dl, dx)))
    return parts


def halves_kernel(behind_ref, ahead_ref, *refs):
    first_ref, second_ref = refs[-2:]
    rows = first_ref.shape[0]
    first_ref[...] = behind_ref[:rows, :]
    second_ref[...] = ahead_ref[rows:, :]


def halves(behind, ahead, after):
    rows, columns = behind.shape
    return pl.pallas_call(
        halves_kernel,
        out_shape=(jax.ShapeDtypeStruct((rows // 2, columns), behind.dtype),) * 2,
        in_specs=[VMEM, VMEM] + [ANY] * len(after),
        out_specs=(VMEM, VMEM),
        compiler_params=pltpu.CompilerParams(vmem_limit_bytes=4 << 20),
        name="halves",
    )(behind, ahead, *after)


def both_ways(own, axis):
    return send(own, **{axis: 1}), send(own, **{axis: -1})


def body(query_grads, doc_grads, out_basis, in_basis, eigenvalues, damping):
    place = jnp.stack([lax.axis_index("example"), lax.axis_index("layer")])

    own, docs = query_grads[0], doc_grads[0]
    docs_there = send(docs, dc=1)

    near = both_ways(own, "dz")
    row = pack(in_basis[0], eigenvalues[0], out_basis[0])
    pair = join([row, send(row, dc=1)], [])
    column = [send(pair, dy=d) for d in range(1, NY)]
    plane = join([pair] + column, near)
    pieces = [plane] + [send(plane, dz=d) for d in range(1, NZ)]
    tables = prepare(place, damping, pieces, [])

    cut = halves(*near, pieces[1:3])
    far = send(cut[0], dz=1), send(cut[1], dz=-1)

    side = rotate(tables, (own, *near), [cut[0]])
    side_y = both_ways(side, "dy")
    other = rotate(tables, far, [side], 20_000_000_000)
    other_y = both_ways(other, "dy")

    docs_other = held(docs_there, [other])

    def scored(blocks, after):
        conditioned = join(blocks, after)
        theirs = send(scores_of(conditioned, docs_other), dc=1)
        return [scores_of(conditioned, docs), theirs]

    parts = scored((side, other), [docs_other])

    low = join([side_y[1]], parts[:1], [(ROWS, 3 * ROWS)])
    high = join([side_y[0], other_y[0]], parts[:1], [(0, ROWS), (0, ROWS)])
    side_far = send(high, dy=1), send(low, dy=-1)
    parts += scored((*side_y, *other_y), [high, low])
    parts += scored(side_far, parts[2:3])

    offsets = [
        [(0, 0), (0, 1), (0, -1), (0, 2)],
        [(1, 0), (1, 1), (1, -1), (-1, 0), (-1, 1), (-1, -1), (1, 2), (-1, 2)],
        [(2, 0), (2, 2), (2, 1), (2, -1)],
    ]
    return finish(spread_over_layers(arrange(place, offsets, parts, [])))


def solution(mesh):
    placed = P("layer", "example", None)
    return jax.shard_map(
        body,
        mesh=mesh,
        in_specs=(placed,) * 5 + (P("layer"),),
        out_specs=P("layer", "example"),
        check_vma=False,
    )
```

```python
import functools
import jax
import jax.numpy as jnp
from jax import lax
from jax.experimental import pallas as pl
from jax.experimental.pallas import tpu as pltpu
from jax.sharding import PartitionSpec as P

NY, NZ, NC = 4, 4, 2
NL, NX = 2, 4
ROWS = 32
CHUNK = 8
OUT, IN = 32, 128
F32, BF16 = jnp.float32, jnp.bfloat16
VMEM = pl.BlockSpec(memory_space=pltpu.VMEM)
SMEM = pl.BlockSpec(memory_space=pltpu.SMEM)
ANY = pl.BlockSpec(memory_space=pl.ANY)
HBM = pl.BlockSpec(memory_space=pltpu.HBM)


def example_shift(dy, dz, dc):
    def place(y, z, c):
        return (y % NY) * NZ * NC + (z % NZ) * NC + c % NC

    return [
        (place(y, z, c), place(y + dy, z + dz, c + dc))
        for y in range(NY)
        for z in range(NZ)
        for c in range(NC)
    ]


def layer_shift(dl, dx):
    return [
        (a * NX + x, ((a + dl) % NL) * NX + (x + dx) % NX) for a in range(NL) for x in range(NX)
    ]


def swap(x, step):
    count = NY * NZ * NC
    return lax.ppermute(x, "example", [(k, k ^ step) for k in range(count)])


def send(x, dy=0, dz=0, dc=0):
    return lax.ppermute(x, "example", example_shift(dy, dz, dc))


def split2(x):
    high = x.astype(BF16)
    return high, (x - high.astype(F32)).astype(BF16)


def mm(a, b, contract=((1,), (0,))):
    return lax.dot_general(a, b, (contract, ((), ())), preferred_element_type=F32)


def coordinates(example):
    return example >> 3, (example >> 1) & 3, example & 1


def held_kernel(x_ref, *refs):
    pltpu.sync_copy(x_ref, refs[-1])


def held(x, after=()):
    return pl.pallas_call(
        held_kernel,
        out_shape=jax.ShapeDtypeStruct(x.shape, x.dtype),
        in_specs=[HBM] + [ANY] * len(after),
        out_specs=VMEM,
        compiler_params=pltpu.CompilerParams(vmem_limit_bytes=16 << 20),
        cost_estimate=pl.CostEstimate(flops=0, bytes_accessed=2 * x.nbytes, transcendentals=0),
        name="held",
    )(x, *after)


def pack_kernel(in_ref, eig_ref, basis_ref, out_ref, in_rows, eig_rows, basis_rows, sems):
    copies = [
        pltpu.make_async_copy(source, target, sems.at[k])
        for k, (source, target) in enumerate(
            ((in_ref, in_rows), (eig_ref, eig_rows), (basis_ref, basis_rows))
        )
    ]
    for copy in copies:
        copy.start()
    out_ref[...] = jnp.zeros_like(out_ref)
    for copy in copies:
        copy.wait()
    out_ref[0:4, :] = in_rows[...]
    out_ref[4:5, :] = eig_rows[...]
    out_ref[5:6, 0:OUT] = basis_rows[...]


def pack(*parts):
    return pl.pallas_call(
        pack_kernel,
        out_shape=jax.ShapeDtypeStruct((8, IN), F32),
        in_specs=[HBM] * 3,
        out_specs=VMEM,
        scratch_shapes=[pltpu.VMEM(p.shape, p.dtype) for p in parts]
        + [pltpu.SemaphoreType.DMA((3,))],
        compiler_params=pltpu.CompilerParams(vmem_limit_bytes=1 << 20),
        name="pack",
    )(*parts)


def join_kernel(ranges, *refs):
    out_ref, at = refs[-1], 0
    for part, (low, high) in zip(refs, ranges):
        out_ref[at : at + high - low, :] = part[low:high, :]
        at += high - low


def join(parts, after, ranges=None):
    ranges = ranges or [(0, p.shape[0]) for p in parts]
    rows = sum(high - low for low, high in ranges)
    columns, dtype = parts[0].shape[1], parts[0].dtype
    return pl.pallas_call(
        functools.partial(join_kernel, ranges),
        out_shape=jax.ShapeDtypeStruct((rows, columns), dtype),
        in_specs=[VMEM] * len(parts) + [ANY] * len(after),
        out_specs=VMEM,
        compiler_params=pltpu.CompilerParams(vmem_limit_bytes=8 << 20),
        name="join",
    )(*parts, *after)


def prepare_kernel(place_ref, damp_ref, *refs):
    pieces, rows = refs[:2], refs[-1]
    left_ref, right_ref, in_ref, back_ref, scale_ref = refs[-6:-1]
    for k in range(NY * NZ * NC):
        apart = (k & 1) + (k >> 1 & 3) * 8 + (k >> 3 & 3) * 2
        at = pl.multiple_of((place_ref[0] ^ apart) * 8, 8)
        rows[pl.ds(at, 8), :] = pieces[k // 16][8 * (k % 16) : 8 * (k % 16) + 8, :]
    table = rows[...]
    high, low = split2(table)
    lowest = (table - high.astype(F32) - low.astype(F32)).astype(BF16)

    def iota(shape, axis):
        return lax.broadcasted_iota(jnp.int32, shape, axis)

    def pick(condition):
        return condition.astype(F32).astype(BF16)

    r, k = iota((IN, 256), 0), iota((IN, 256), 1)
    pick_in = pick(k == (r // 4) * 8 + r % 4)
    basis, rest = mm(pick_in, high), mm(pick_in, low)
    in_ref[...] = jnp.concatenate([basis, rest], axis=0).astype(BF16)
    turned, turned_rest = basis.T, rest.T
    back_ref[...] = jnp.concatenate(
        [
            jnp.concatenate([turned, turned_rest], axis=1),
            jnp.concatenate([turned, jnp.zeros_like(turned)], axis=1),
        ],
        axis=0,
    ).astype(BF16)
    r, k = iota((256, 256), 0), iota((256, 256), 1)
    pick_eig = pick(k == (r // 8) * 8 + 4)
    eig = mm(pick_eig, high) + (mm(pick_eig, low) + mm(pick_eig, lowest))
    scale_ref[...] = 1.0 / (eig + damp_ref[0])
    pick_out = pick(k == (r // 8) * 8 + 5)
    spread = pick(iota((IN, 256), 0) == iota((IN, 256), 1) // 8)
    same = (r % 8 == k % 8).astype(F32)
    for term, part in enumerate((high, low)):
        whole = mm(mm(pick_out, part).astype(BF16), spread) * same
        right_ref[256 * term : 256 * (term + 1), :] = whole.astype(BF16)
        left_ref[256 * term : 256 * (term + 1), :] = whole.T.astype(BF16)


def prepare(place, damping, pieces, after):
    shape = jax.ShapeDtypeStruct
    return pl.pallas_call(
        prepare_kernel,
        out_shape=(
            shape((512, 256), BF16),
            shape((512, 256), BF16),
            shape((2 * IN, IN), BF16),
            shape((2 * IN, 2 * IN), BF16),
            shape((256, IN), F32),
        ),
        in_specs=[SMEM, SMEM] + [VMEM] * len(pieces) + [ANY] * len(after),
        out_specs=(VMEM,) * 5,
        scratch_shapes=[pltpu.VMEM((256, 128), F32)],
        compiler_params=pltpu.CompilerParams(vmem_limit_bytes=16 << 20),
        cost_estimate=pl.CostEstimate(flops=200_000_000, bytes_accessed=1 << 20, transcendentals=0),
        name="prepare",
    )(place, damping, *pieces, *after)


def mix(matrix, x):
    high, low = split2(x)
    both = mm(matrix, high)
    return both[:256] + (both[256:] + mm(matrix[:256], low))


def rotate_chunk(x, left, right, basis, back, scale):
    count = 2 * len(x)
    tall = jnp.concatenate(
        [piece[:, IN * i : IN * (i + 1)] for piece in x for i in range(OUT)], axis=0
    )
    half = mm(jnp.concatenate([tall, tall], axis=1), basis)
    half = half.reshape(count // 2, OUT, 2, 8, IN)
    side = jnp.concatenate(
        [half[g // 2, :, g % 2].reshape(OUT * 8, IN) for g in range(count)], axis=1
    )
    rotated = mix(left, side)
    scaled = jnp.concatenate(
        [rotated[:, IN * g : IN * (g + 1)] * scale for g in range(count)], axis=0
    )
    restored = mm(jnp.concatenate(split2(scaled), axis=1), back)
    restored = restored[:, :IN] + restored[:, IN:]
    side = jnp.concatenate([restored[256 * g : 256 * (g + 1)] for g in range(count)], axis=1)
    return mix(right, side)


def rotate_kernel(most, count, left_ref, right_ref, in_ref, back_ref, scale_ref, *refs):
    blocks, out_ref = refs[:count], refs[-1]
    pieces = [(b, at) for b in blocks for at in range(0, b.shape[0], 16)]
    step = -(-len(pieces) // -(-len(pieces) // most))
    for first in range(0, len(pieces), step):
        chunk = pieces[first : first + step]
        done = rotate_chunk(
            [b[at : at + 16, :] for b, at in chunk],
            left_ref[...],
            right_ref[...],
            in_ref[...],
            back_ref[...],
            scale_ref[...],
        )
        for p in range(len(chunk)):
            to = 16 * (first + p)
            for i in range(OUT):
                rows = done[8 * i : 8 * i + 8, 2 * IN * p : 2 * IN * (p + 1)]
                rows = jnp.concatenate([rows[:, :IN], rows[:, IN:]], axis=0)
                out_ref[to : to + 16, IN * i : IN * (i + 1)] = rows.astype(BF16)


def rotate(tables, blocks, after, flops=0):
    rows = sum(b.shape[0] for b in blocks)
    width = blocks[0].shape[1]
    return pl.pallas_call(
        functools.partial(rotate_kernel, CHUNK, len(blocks)),
        out_shape=jax.ShapeDtypeStruct((rows, width), BF16),
        in_specs=[VMEM] * (5 + len(blocks)) + [ANY] * len(after),
        out_specs=VMEM,
        compiler_params=pltpu.CompilerParams(vmem_limit_bytes=32 << 20),
        cost_estimate=pl.CostEstimate(flops=flops, bytes_accessed=0, transcendentals=0),
        name="rotate",
    )(*tables, *blocks, *after)


def scores_of(conditioned, documents):
    return lax.dot_general(
        conditioned, documents, (((1,), (1,)), ((), ())), preferred_element_type=F32
    ).astype(BF16)


def arrange_kernel(offsets, place_ref, *refs):
    parts, out_ref = refs[: 2 * len(offsets)], refs[-1]
    y, z, c = coordinates(place_ref[0])
    layer = place_ref[1]
    for k, part in enumerate(parts):
        kind = c ^ (k % 2)
        for at, (dy, dz) in enumerate(offsets[k // 2]):
            from_z = (z - dz) & 3
            to = ((y - dy) & 3) * 2 + (from_z >> 1)
            turn = ((to ^ layer) & 4) + ((to - layer) & 3)
            out_ref[turn * 4 + (from_z & 1) * 2 + kind] = part[ROWS * at : ROWS * (at + 1), :]


def arrange(place, offsets, parts, after):
    count = sum(p.shape[0] for p in parts) // ROWS
    columns = parts[0].shape[1]
    return pl.pallas_call(
        functools.partial(arrange_kernel, offsets),
        out_shape=jax.ShapeDtypeStruct((count, ROWS, columns), BF16),
        in_specs=[SMEM] + [VMEM] * len(parts) + [ANY] * len(after),
        out_specs=VMEM,
        compiler_params=pltpu.CompilerParams(vmem_limit_bytes=16 << 20),
        cost_estimate=pl.CostEstimate(
            flops=0, bytes_accessed=count * ROWS * columns * 4, transcendentals=0
        ),
        name="arrange",
    )(place, *parts, *after)


def finish_kernel(*refs):
    total = refs[0][...].astype(F32)
    for part in refs[1:-1]:
        total += part[...].astype(F32)
    refs[-1][...] = total


def finish(parts):
    return pl.pallas_call(
        finish_kernel,
        out_shape=jax.ShapeDtypeStruct(parts[0].shape, F32),
        in_specs=[VMEM] * len(parts),
        out_specs=VMEM,
        compiler_params=pltpu.CompilerParams(vmem_limit_bytes=8 << 20),
        name="finish",
    )(*parts)


def spread_over_layers(ready):
    ready = ready.reshape(NL * NX, 4 * ROWS, ready.shape[-1])
    parts = [ready[0]]
    for dl, dx in ((1, 2), (0, 2), (1, 1), (1, 3), (1, 0), (0, 1), (0, 3)):
        parts.append(lax.ppermute(ready[dl * NX + dx], "layer", layer_shift(dl, dx)))
    return parts


def halves_kernel(behind_ref, ahead_ref, *refs):
    first_ref, second_ref = refs[-2:]
    rows = first_ref.shape[0]
    first_ref[...] = behind_ref[:rows, :]
    second_ref[...] = ahead_ref[rows:, :]


def halves(behind, ahead, after):
    rows, columns = behind.shape
    return pl.pallas_call(
        halves_kernel,
        out_shape=(jax.ShapeDtypeStruct((rows // 2, columns), behind.dtype),) * 2,
        in_specs=[VMEM, VMEM] + [ANY] * len(after),
        out_specs=(VMEM, VMEM),
        compiler_params=pltpu.CompilerParams(vmem_limit_bytes=4 << 20),
        name="halves",
    )(behind, ahead, *after)


def both_ways(own, axis):
    return send(own, **{axis: 1}), send(own, **{axis: -1})


def body(query_grads, doc_grads, out_basis, in_basis, eigenvalues, damping):
    place = jnp.stack([lax.axis_index("example"), lax.axis_index("layer")])

    own, docs = query_grads[0], doc_grads[0]
    docs_there = send(docs, dc=1)

    near = both_ways(own, "dz")
    row = pack(in_basis[0], eigenvalues[0], out_basis[0])
    rows = join([row, swap(row, 1)], [])
    for step in (8, 16, 2):
        rows = join([rows, swap(rows, step)], [])
    last = swap(rows, 4)
    tables = prepare(place, damping, [rows, last], [])

    cut = halves(*near, [last])
    far = send(cut[0], dz=1), send(cut[1], dz=-1)

    side = rotate(tables, (own, *near), [cut[0]])
    side_y = both_ways(side, "dy")
    other = rotate(tables, far, [side], 20_000_000_000)
    other_y = both_ways(other, "dy")

    docs_other = held(docs_there, [other])

    def scored(blocks, after):
        conditioned = join(blocks, after)
        theirs = send(scores_of(conditioned, docs_other), dc=1)
        return [scores_of(conditioned, docs), theirs]

    parts = scored((side, other), [docs_other])

    low = join([side_y[1]], parts[:1], [(ROWS, 3 * ROWS)])
    high = join([side_y[0], other_y[0]], parts[:1], [(0, ROWS), (0, ROWS)])
    side_far = send(high, dy=1), send(low, dy=-1)
    parts += scored((*side_y, *other_y), [high, low])
    parts += scored(side_far, parts[2:3])

    offsets = [
        [(0, 0), (0, 1), (0, -1), (0, 2)],
        [(1, 0), (1, 1), (1, -1), (-1, 0), (-1, 1), (-1, -1), (1, 2), (-1, 2)],
        [(2, 0), (2, 2), (2, 1), (2, -1)],
    ]
    return finish(spread_over_layers(arrange(place, offsets, parts, [])))


def solution(mesh):
    placed = P("layer", "example", None)
    return jax.shard_map(
        body,
        mesh=mesh,
        in_specs=(placed,) * 5 + (P("layer"),),
        out_specs=P("layer", "example"),
        check_vma=False,
    )
```

```python
import functools
import jax
import jax.numpy as jnp
from jax import lax
from jax.experimental import pallas as pl
from jax.experimental.pallas import tpu as pltpu
from jax.sharding import PartitionSpec as P

NY, NZ, NC = 4, 4, 2
NL, NX = 2, 4
ROWS = 32
CHUNK = 8
OUT, IN = 32, 128
F32, BF16 = jnp.float32, jnp.bfloat16
VMEM = pl.BlockSpec(memory_space=pltpu.VMEM)
SMEM = pl.BlockSpec(memory_space=pltpu.SMEM)
ANY = pl.BlockSpec(memory_space=pl.ANY)
HBM = pl.BlockSpec(memory_space=pltpu.HBM)


def example_shift(dy, dz, dc):
    def place(y, z, c):
        return (y % NY) * NZ * NC + (z % NZ) * NC + c % NC

    return [
        (place(y, z, c), place(y + dy, z + dz, c + dc))
        for y in range(NY)
        for z in range(NZ)
        for c in range(NC)
    ]


def layer_shift(dl, dx):
    layers = NL * NX

    def place(e, a, x):
        return e * layers + (a % NL) * NX + x % NX

    return [
        (place(e, a, x), place(e, a + dl, x + dx * (1 - 2 * (e % NC))))
        for e in range(NY * NZ * NC)
        for a in range(NL)
        for x in range(NX)
    ]


def to_layer(x, dl, dx):
    return lax.ppermute(x, ("example", "layer"), layer_shift(dl, dx))


def send(x, dy=0, dz=0, dc=0):
    return lax.ppermute(x, "example", example_shift(dy, dz, dc))


def split2(x):
    high = x.astype(BF16)
    return high, (x - high.astype(F32)).astype(BF16)


def mm(a, b, contract=((1,), (0,))):
    return lax.dot_general(a, b, (contract, ((), ())), preferred_element_type=F32)


def coordinates(example):
    return example >> 3, (example >> 1) & 3, example & 1


def held_kernel(x_ref, *refs):
    pltpu.sync_copy(x_ref, refs[-1])


def held(x, after=()):
    return pl.pallas_call(
        held_kernel,
        out_shape=jax.ShapeDtypeStruct(x.shape, x.dtype),
        in_specs=[HBM] + [ANY] * len(after),
        out_specs=VMEM,
        compiler_params=pltpu.CompilerParams(vmem_limit_bytes=16 << 20),
        cost_estimate=pl.CostEstimate(flops=0, bytes_accessed=2 * x.nbytes, transcendentals=0),
        name="held",
    )(x, *after)


def pack_kernel(in_ref, eig_ref, basis_ref, out_ref, in_rows, eig_rows, basis_rows, sems):
    copies = [
        pltpu.make_async_copy(source, target, sems.at[k])
        for k, (source, target) in enumerate(
            ((in_ref, in_rows), (eig_ref, eig_rows), (basis_ref, basis_rows))
        )
    ]
    for copy in copies:
        copy.start()
    out_ref[...] = jnp.zeros_like(out_ref)
    for copy in copies:
        copy.wait()
    out_ref[0:4, :] = in_rows[...]
    out_ref[4:5, :] = eig_rows[...]
    out_ref[5:6, 0:OUT] = basis_rows[...]


def pack(*parts):
    return pl.pallas_call(
        pack_kernel,
        out_shape=jax.ShapeDtypeStruct((8, IN), F32),
        in_specs=[HBM] * 3,
        out_specs=VMEM,
        scratch_shapes=[pltpu.VMEM(p.shape, p.dtype) for p in parts]
        + [pltpu.SemaphoreType.DMA((3,))],
        compiler_params=pltpu.CompilerParams(vmem_limit_bytes=1 << 20),
        name="pack",
    )(*parts)


def join_kernel(ranges, *refs):
    out_ref, at = refs[-1], 0
    for part, (low, high) in zip(refs, ranges):
        out_ref[at : at + high - low, :] = part[low:high, :]
        at += high - low


def join(parts, after, ranges=None):
    ranges = ranges or [(0, p.shape[0]) for p in parts]
    rows = sum(high - low for low, high in ranges)
    columns, dtype = parts[0].shape[1], parts[0].dtype
    return pl.pallas_call(
        functools.partial(join_kernel, ranges),
        out_shape=jax.ShapeDtypeStruct((rows, columns), dtype),
        in_specs=[VMEM] * len(parts) + [ANY] * len(after),
        out_specs=VMEM,
        compiler_params=pltpu.CompilerParams(vmem_limit_bytes=8 << 20),
        name="join",
    )(*parts, *after)


def prepare_kernel(place_ref, damp_ref, *refs):
    pieces, rows = refs[:NZ], refs[-1]
    left_ref, right_ref, in_ref, back_ref, scale_ref = refs[-6:-1]
    y, z, c = coordinates(place_ref[0])
    for dz in range(NZ):
        for dy in range(NY):
            for dc in range(NC):
                owner = ((y - dy) & 3) * 8 + ((z - dz) & 3) * 2 + (c ^ dc)
                k = dy * NC + dc
                piece = pieces[dz][8 * k : 8 * k + 8, :]
                rows[pl.ds(pl.multiple_of(owner * 8, 8), 8), :] = piece
    table = rows[...]
    high, low = split2(table)
    lowest = (table - high.astype(F32) - low.astype(F32)).astype(BF16)

    def iota(shape, axis):
        return lax.broadcasted_iota(jnp.int32, shape, axis)

    def pick(condition):
        return condition.astype(F32).astype(BF16)

    r, k = iota((IN, 256), 0), iota((IN, 256), 1)
    pick_in = pick(k == (r // 4) * 8 + r % 4)
    basis, rest = mm(pick_in, high), mm(pick_in, low)
    in_ref[...] = jnp.concatenate([basis, rest], axis=0).astype(BF16)
    turned, turned_rest = basis.T, rest.T
    back_ref[...] = jnp.concatenate(
        [
            jnp.concatenate([turned, turned_rest], axis=1),
            jnp.concatenate([turned, jnp.zeros_like(turned)], axis=1),
        ],
        axis=0,
    ).astype(BF16)
    r, k = iota((256, 256), 0), iota((256, 256), 1)
    pick_eig = pick(k == (r // 8) * 8 + 4)
    eig = mm(pick_eig, high) + (mm(pick_eig, low) + mm(pick_eig, lowest))
    scale_ref[...] = 1.0 / (eig + damp_ref[0])
    pick_out = pick(k == (r // 8) * 8 + 5)
    spread = pick(iota((IN, 256), 0) == iota((IN, 256), 1) // 8)
    same = (r % 8 == k % 8).astype(F32)
    for term, part in enumerate((high, low)):
        whole = mm(mm(pick_out, part).astype(BF16), spread) * same
        right_ref[256 * term : 256 * (term + 1), :] = whole.astype(BF16)
        left_ref[256 * term : 256 * (term + 1), :] = whole.T.astype(BF16)


def prepare(place, damping, pieces, after):
    shape = jax.ShapeDtypeStruct
    return pl.pallas_call(
        prepare_kernel,
        out_shape=(
            shape((512, 256), BF16),
            shape((512, 256), BF16),
            shape((2 * IN, IN), BF16),
            shape((2 * IN, 2 * IN), BF16),
            shape((256, IN), F32),
        ),
        in_specs=[SMEM, SMEM] + [VMEM] * NZ + [ANY] * len(after),
        out_specs=(VMEM,) * 5,
        scratch_shapes=[pltpu.VMEM((256, 128), F32)],
        compiler_params=pltpu.CompilerParams(vmem_limit_bytes=16 << 20),
        cost_estimate=pl.CostEstimate(flops=200_000_000, bytes_accessed=1 << 20, transcendentals=0),
        name="prepare",
    )(place, damping, *pieces, *after)


def mix(matrix, x):
    high, low = split2(x)
    both = mm(matrix, high)
    return both[:256] + (both[256:] + mm(matrix[:256], low))


def rotate_chunk(x, left, right, basis, back, scale):
    count = 2 * len(x)
    tall = jnp.concatenate(
        [piece[:, IN * i : IN * (i + 1)] for piece in x for i in range(OUT)], axis=0
    )
    half = mm(jnp.concatenate([tall, tall], axis=1), basis)
    half = half.reshape(count // 2, OUT, 2, 8, IN)
    side = jnp.concatenate(
        [half[g // 2, :, g % 2].reshape(OUT * 8, IN) for g in range(count)], axis=1
    )
    rotated = mix(left, side)
    scaled = jnp.concatenate(
        [rotated[:, IN * g : IN * (g + 1)] * scale for g in range(count)], axis=0
    )
    restored = mm(jnp.concatenate(split2(scaled), axis=1), back)
    restored = restored[:, :IN] + restored[:, IN:]
    side = jnp.concatenate([restored[256 * g : 256 * (g + 1)] for g in range(count)], axis=1)
    return mix(right, side)


def rotate_kernel(most, count, left_ref, right_ref, in_ref, back_ref, scale_ref, *refs):
    blocks, out_ref = refs[:count], refs[-1]
    pieces = [(b, at) for b in blocks for at in range(0, b.shape[0], 16)]
    step = -(-len(pieces) // -(-len(pieces) // most))
    for first in range(0, len(pieces), step):
        chunk = pieces[first : first + step]
        done = rotate_chunk(
            [b[at : at + 16, :] for b, at in chunk],
            left_ref[...],
            right_ref[...],
            in_ref[...],
            back_ref[...],
            scale_ref[...],
        )
        for p in range(len(chunk)):
            to = 16 * (first + p)
            for i in range(OUT):
                rows = done[8 * i : 8 * i + 8, 2 * IN * p : 2 * IN * (p + 1)]
                rows = jnp.concatenate([rows[:, :IN], rows[:, IN:]], axis=0)
                out_ref[to : to + 16, IN * i : IN * (i + 1)] = rows.astype(BF16)


def rotate(tables, blocks, after, flops=0):
    rows = sum(b.shape[0] for b in blocks)
    width = blocks[0].shape[1]
    return pl.pallas_call(
        functools.partial(rotate_kernel, CHUNK, len(blocks)),
        out_shape=jax.ShapeDtypeStruct((rows, width), BF16),
        in_specs=[VMEM] * (5 + len(blocks)) + [ANY] * len(after),
        out_specs=VMEM,
        compiler_params=pltpu.CompilerParams(vmem_limit_bytes=32 << 20),
        cost_estimate=pl.CostEstimate(flops=flops, bytes_accessed=0, transcendentals=0),
        name="rotate",
    )(*tables, *blocks, *after)


def scores_of(conditioned, documents):
    return lax.dot_general(
        conditioned, documents, (((1,), (1,)), ((), ())), preferred_element_type=F32
    ).astype(BF16)


def arrange_kernel(offsets, place_ref, *refs):
    parts, out_ref = refs[: 2 * len(offsets)], refs[-1]
    y, z, c = coordinates(place_ref[0])
    layer = place_ref[1]
    for k, part in enumerate(parts):
        kind = c ^ (k % 2)
        for at, (dy, dz) in enumerate(offsets[k // 2]):
            from_z = (z - dz) & 3
            to = ((y - dy) & 3) * 2 + (from_z >> 1)
            ahead = ((to - layer) * (1 - 2 * c)) & 3
            turn = (ahead ^ 2) * 2 + (((to ^ layer) >> 2) & 1)
            out_ref[turn * 4 + (from_z & 1) * 2 + kind] = part[ROWS * at : ROWS * (at + 1), :]


def arrange(place, offsets, parts, after):
    count = sum(p.shape[0] for p in parts) // ROWS
    columns = parts[0].shape[1]
    return pl.pallas_call(
        functools.partial(arrange_kernel, offsets),
        out_shape=jax.ShapeDtypeStruct((count, ROWS, columns), BF16),
        in_specs=[SMEM] + [VMEM] * len(parts) + [ANY] * len(after),
        out_specs=VMEM,
        compiler_params=pltpu.CompilerParams(vmem_limit_bytes=16 << 20),
        cost_estimate=pl.CostEstimate(
            flops=0, bytes_accessed=count * ROWS * columns * 4, transcendentals=0
        ),
        name="arrange",
    )(place, *parts, *after)


def finish_kernel(*refs):
    total = refs[0][...].astype(F32)
    for part in refs[1:-1]:
        total += part[...].astype(F32)
    refs[-1][...] = total


def finish(parts):
    return pl.pallas_call(
        finish_kernel,
        out_shape=jax.ShapeDtypeStruct(parts[0].shape, F32),
        in_specs=[VMEM] * len(parts),
        out_specs=VMEM,
        compiler_params=pltpu.CompilerParams(vmem_limit_bytes=8 << 20),
        name="finish",
    )(*parts)


def spread_over_layers(ready):
    ready = ready.reshape(NL * NX, 4 * ROWS, ready.shape[-1])
    passing = to_layer(ready[0:2], 0, 1)
    parts = [ready[4], to_layer(ready[5], 1, 0)]
    parts += [to_layer(ready[2], 0, 3), to_layer(ready[3], 1, 3)]
    joint = (ready[6:8].astype(F32) + passing.astype(F32)).astype(BF16)
    return parts + [to_layer(joint[0], 0, 1), to_layer(joint[1], 1, 1)]


def halves_kernel(behind_ref, ahead_ref, *refs):
    first_ref, second_ref = refs[-2:]
    rows = first_ref.shape[0]
    first_ref[...] = behind_ref[:rows, :]
    second_ref[...] = ahead_ref[rows:, :]


def halves(behind, ahead, after):
    rows, columns = behind.shape
    return pl.pallas_call(
        halves_kernel,
        out_shape=(jax.ShapeDtypeStruct((rows // 2, columns), behind.dtype),) * 2,
        in_specs=[VMEM, VMEM] + [ANY] * len(after),
        out_specs=(VMEM, VMEM),
        compiler_params=pltpu.CompilerParams(vmem_limit_bytes=4 << 20),
        name="halves",
    )(behind, ahead, *after)


def both_ways(own, axis):
    return send(own, **{axis: 1}), send(own, **{axis: -1})


def body(query_grads, doc_grads, out_basis, in_basis, eigenvalues, damping):
    place = jnp.stack([lax.axis_index("example"), lax.axis_index("layer")])

    own, docs = query_grads[0], doc_grads[0]
    docs_there = send(docs, dc=1)

    near = both_ways(own, "dz")
    row = pack(in_basis[0], eigenvalues[0], out_basis[0])
    pair = join([row, send(row, dc=1)], [])
    column = [send(pair, dy=d) for d in range(1, NY)]
    plane = join([pair] + column, [docs_there])
    pieces = [plane] + [send(plane, dz=d) for d in range(1, NZ)]
    tables = prepare(place, damping, pieces, [])

    cut = halves(*near, pieces[1:3])
    far = send(cut[0], dz=1), send(cut[1], dz=-1)

    side = rotate(tables, (own, *near), [cut[0]])
    side_y = both_ways(side, "dy")
    other = rotate(tables, far, [side], 20_000_000_000)
    other_y = both_ways(other, "dy")

    low = join([side_y[1]], [], [(ROWS, 3 * ROWS)])
    high = join([side_y[0], other_y[0]], [], [(0, ROWS), (0, ROWS)])
    side_far = send(high, dy=1), send(low, dy=-1)

    docs_other = held(docs_there, [other])

    offsets = [
        [(0, 0), (0, 1), (0, -1), (0, 2)],
        [(1, 0), (1, 1), (1, -1), (-1, 0), (-1, 1), (-1, -1), (1, 2), (-1, 2)],
        [(2, 0), (2, 2), (2, 1), (2, -1)],
    ]
    parts = []
    for blocks, after in (((side, other), [docs_other]), ((*side_y, *other_y), [high, low]), (side_far, [])):
        conditioned = join(blocks, after + parts[-2:-1])
        theirs = send(scores_of(conditioned, docs_other), dc=1)
        parts += [scores_of(conditioned, docs), theirs]
    return finish(spread_over_layers(arrange(place, offsets, parts, [])))


def solution(mesh):
    placed = P("layer", "example", None)
    return jax.shard_map(
        body,
        mesh=mesh,
        in_specs=(placed,) * 5 + (P("layer"),),
        out_specs=P("layer", "example"),
        check_vma=False,
    )
```

```python
import functools
import jax
import jax.numpy as jnp
from jax import lax
from jax.experimental import pallas as pl
from jax.experimental.pallas import tpu as pltpu
from jax.sharding import PartitionSpec as P

NY, NZ, NC = 4, 4, 2
NL, NX = 2, 4
ROWS = 32
CHUNK = 8
OUT, IN = 32, 128
F32, BF16 = jnp.float32, jnp.bfloat16
VMEM = pl.BlockSpec(memory_space=pltpu.VMEM)
SMEM = pl.BlockSpec(memory_space=pltpu.SMEM)
ANY = pl.BlockSpec(memory_space=pl.ANY)
HBM = pl.BlockSpec(memory_space=pltpu.HBM)


def example_shift(dy, dz, dc):
    def place(y, z, c):
        return (y % NY) * NZ * NC + (z % NZ) * NC + c % NC

    return [
        (place(y, z, c), place(y + dy, z + dz, c + dc))
        for y in range(NY)
        for z in range(NZ)
        for c in range(NC)
    ]


def layer_shift(dl, dx):
    layers = NL * NX

    def place(e, a, x):
        return e * layers + (a % NL) * NX + x % NX

    return [
        (place(e, a, x), place(e, a + dl, x + dx * (1 - 2 * (e % NC))))
        for e in range(NY * NZ * NC)
        for a in range(NL)
        for x in range(NX)
    ]


def to_layer(x, dl, dx):
    return lax.ppermute(x, ("example", "layer"), layer_shift(dl, dx))


def send(x, dy=0, dz=0, dc=0):
    return lax.ppermute(x, "example", example_shift(dy, dz, dc))


def split2(x):
    high = x.astype(BF16)
    return high, (x - high.astype(F32)).astype(BF16)


def mm(a, b, contract=((1,), (0,))):
    return lax.dot_general(a, b, (contract, ((), ())), preferred_element_type=F32)


def coordinates(example):
    return example >> 3, (example >> 1) & 3, example & 1


def held_kernel(x_ref, *refs):
    pltpu.sync_copy(x_ref, refs[-1])


def held(x, after=()):
    return pl.pallas_call(
        held_kernel,
        out_shape=jax.ShapeDtypeStruct(x.shape, x.dtype),
        in_specs=[HBM] + [ANY] * len(after),
        out_specs=VMEM,
        compiler_params=pltpu.CompilerParams(vmem_limit_bytes=16 << 20),
        cost_estimate=pl.CostEstimate(flops=0, bytes_accessed=2 * x.nbytes, transcendentals=0),
        name="held",
    )(x, *after)


def pack_kernel(in_ref, eig_ref, basis_ref, out_ref, in_rows, eig_rows, basis_rows, sems):
    copies = [
        pltpu.make_async_copy(source, target, sems.at[k])
        for k, (source, target) in enumerate(
            ((in_ref, in_rows), (eig_ref, eig_rows), (basis_ref, basis_rows))
        )
    ]
    for copy in copies:
        copy.start()
    out_ref[...] = jnp.zeros_like(out_ref)
    for copy in copies:
        copy.wait()
    out_ref[0:4, :] = in_rows[...]
    out_ref[4:5, :] = eig_rows[...]
    out_ref[5:6, 0:OUT] = basis_rows[...]


def pack(*parts):
    return pl.pallas_call(
        pack_kernel,
        out_shape=jax.ShapeDtypeStruct((8, IN), F32),
        in_specs=[HBM] * 3,
        out_specs=VMEM,
        scratch_shapes=[pltpu.VMEM(p.shape, p.dtype) for p in parts]
        + [pltpu.SemaphoreType.DMA((3,))],
        compiler_params=pltpu.CompilerParams(vmem_limit_bytes=1 << 20),
        name="pack",
    )(*parts)


def join_kernel(ranges, *refs):
    out_ref, at = refs[-1], 0
    for part, (low, high) in zip(refs, ranges):
        out_ref[at : at + high - low, :] = part[low:high, :]
        at += high - low


def join(parts, after, ranges=None):
    ranges = ranges or [(0, p.shape[0]) for p in parts]
    rows = sum(high - low for low, high in ranges)
    columns, dtype = parts[0].shape[1], parts[0].dtype
    return pl.pallas_call(
        functools.partial(join_kernel, ranges),
        out_shape=jax.ShapeDtypeStruct((rows, columns), dtype),
        in_specs=[VMEM] * len(parts) + [ANY] * len(after),
        out_specs=VMEM,
        compiler_params=pltpu.CompilerParams(vmem_limit_bytes=8 << 20),
        name="join",
    )(*parts, *after)


def prepare_kernel(place_ref, damp_ref, *refs):
    pieces, rows = refs[:NZ], refs[-1]
    left_ref, right_ref, in_ref, back_ref, scale_ref = refs[-6:-1]
    y, z, c = coordinates(place_ref[0])
    for dz in range(NZ):
        for dy in range(NY):
            for dc in range(NC):
                owner = ((y - dy) & 3) * 8 + ((z - dz) & 3) * 2 + (c ^ dc)
                k = dy * NC + dc
                piece = pieces[dz][8 * k : 8 * k + 8, :]
                rows[pl.ds(pl.multiple_of(owner * 8, 8), 8), :] = piece
    table = rows[...]
    high, low = split2(table)
    lowest = (table - high.astype(F32) - low.astype(F32)).astype(BF16)

    def iota(shape, axis):
        return lax.broadcasted_iota(jnp.int32, shape, axis)

    def pick(condition):
        return condition.astype(F32).astype(BF16)

    r, k = iota((IN, 256), 0), iota((IN, 256), 1)
    pick_in = pick(k == (r // 4) * 8 + r % 4)
    basis, rest = mm(pick_in, high), mm(pick_in, low)
    in_ref[...] = jnp.concatenate([basis, rest], axis=0).astype(BF16)
    turned, turned_rest = basis.T, rest.T
    back_ref[...] = jnp.concatenate(
        [
            jnp.concatenate([turned, turned_rest], axis=1),
            jnp.concatenate([turned, jnp.zeros_like(turned)], axis=1),
        ],
        axis=0,
    ).astype(BF16)
    r, k = iota((256, 256), 0), iota((256, 256), 1)
    pick_eig = pick(k == (r // 8) * 8 + 4)
    eig = mm(pick_eig, high) + (mm(pick_eig, low) + mm(pick_eig, lowest))
    scale_ref[...] = 1.0 / (eig + damp_ref[0])
    pick_out = pick(k == (r // 8) * 8 + 5)
    spread = pick(iota((IN, 256), 0) == iota((IN, 256), 1) // 8)
    same = (r % 8 == k % 8).astype(F32)
    for term, part in enumerate((high, low)):
        whole = mm(mm(pick_out, part).astype(BF16), spread) * same
        right_ref[256 * term : 256 * (term + 1), :] = whole.astype(BF16)
        left_ref[256 * term : 256 * (term + 1), :] = whole.T.astype(BF16)


def prepare(place, damping, pieces, after):
    shape = jax.ShapeDtypeStruct
    return pl.pallas_call(
        prepare_kernel,
        out_shape=(
            shape((512, 256), BF16),
            shape((512, 256), BF16),
            shape((2 * IN, IN), BF16),
            shape((2 * IN, 2 * IN), BF16),
            shape((256, IN), F32),
        ),
        in_specs=[SMEM, SMEM] + [VMEM] * NZ + [ANY] * len(after),
        out_specs=(VMEM,) * 5,
        scratch_shapes=[pltpu.VMEM((256, 128), F32)],
        compiler_params=pltpu.CompilerParams(vmem_limit_bytes=16 << 20),
        cost_estimate=pl.CostEstimate(flops=200_000_000, bytes_accessed=1 << 20, transcendentals=0),
        name="prepare",
    )(place, damping, *pieces, *after)


def mix(matrix, x):
    high, low = split2(x)
    both = mm(matrix, high)
    return both[:256] + (both[256:] + mm(matrix[:256], low))


def rotate_chunk(x, left, right, basis, back, scale):
    count = 2 * len(x)
    tall = jnp.concatenate(
        [piece[:, IN * i : IN * (i + 1)] for piece in x for i in range(OUT)], axis=0
    )
    half = mm(jnp.concatenate([tall, tall], axis=1), basis)
    half = half.reshape(count // 2, OUT, 2, 8, IN)
    side = jnp.concatenate(
        [half[g // 2, :, g % 2].reshape(OUT * 8, IN) for g in range(count)], axis=1
    )
    rotated = mix(left, side)
    scaled = jnp.concatenate(
        [rotated[:, IN * g : IN * (g + 1)] * scale for g in range(count)], axis=0
    )
    restored = mm(jnp.concatenate(split2(scaled), axis=1), back)
    restored = restored[:, :IN] + restored[:, IN:]
    side = jnp.concatenate([restored[256 * g : 256 * (g + 1)] for g in range(count)], axis=1)
    return mix(right, side)


def rotate_kernel(most, count, left_ref, right_ref, in_ref, back_ref, scale_ref, *refs):
    blocks, out_ref = refs[:count], refs[-1]
    pieces = [(b, at) for b in blocks for at in range(0, b.shape[0], 16)]
    step = -(-len(pieces) // -(-len(pieces) // most))
    for first in range(0, len(pieces), step):
        chunk = pieces[first : first + step]
        done = rotate_chunk(
            [b[at : at + 16, :] for b, at in chunk],
            left_ref[...],
            right_ref[...],
            in_ref[...],
            back_ref[...],
            scale_ref[...],
        )
        for p in range(len(chunk)):
            to = 16 * (first + p)
            for i in range(OUT):
                rows = done[8 * i : 8 * i + 8, 2 * IN * p : 2 * IN * (p + 1)]
                rows = jnp.concatenate([rows[:, :IN], rows[:, IN:]], axis=0)
                out_ref[to : to + 16, IN * i : IN * (i + 1)] = rows.astype(BF16)


def rotate(tables, blocks, after, flops=0):
    rows = sum(b.shape[0] for b in blocks)
    width = blocks[0].shape[1]
    return pl.pallas_call(
        functools.partial(rotate_kernel, CHUNK, len(blocks)),
        out_shape=jax.ShapeDtypeStruct((rows, width), BF16),
        in_specs=[VMEM] * (5 + len(blocks)) + [ANY] * len(after),
        out_specs=VMEM,
        compiler_params=pltpu.CompilerParams(vmem_limit_bytes=32 << 20),
        cost_estimate=pl.CostEstimate(flops=flops, bytes_accessed=0, transcendentals=0),
        name="rotate",
    )(*tables, *blocks, *after)


def scores_of(conditioned, documents):
    return lax.dot_general(
        conditioned, documents, (((1,), (1,)), ((), ())), preferred_element_type=F32
    ).astype(BF16)


def arrange_kernel(offsets, place_ref, *refs):
    parts, out_ref = refs[: 2 * len(offsets)], refs[-1]
    y, z, c = coordinates(place_ref[0])
    layer = place_ref[1]
    for k, part in enumerate(parts):
        kind = c ^ (k % 2)
        for at, (dy, dz) in enumerate(offsets[k // 2]):
            from_z = (z - dz) & 3
            to = ((y - dy) & 3) * 2 + (from_z >> 1)
            ahead = ((to - layer) * (1 - 2 * c)) & 3
            turn = (ahead ^ 2) * 2 + (((to ^ layer) >> 2) & 1)
            out_ref[turn * 4 + (from_z & 1) * 2 + kind] = part[ROWS * at : ROWS * (at + 1), :]


def arrange(place, offsets, parts, after):
    count = sum(p.shape[0] for p in parts) // ROWS
    columns = parts[0].shape[1]
    return pl.pallas_call(
        functools.partial(arrange_kernel, offsets),
        out_shape=jax.ShapeDtypeStruct((count, ROWS, columns), BF16),
        in_specs=[SMEM] + [VMEM] * len(parts) + [ANY] * len(after),
        out_specs=VMEM,
        compiler_params=pltpu.CompilerParams(vmem_limit_bytes=16 << 20),
        cost_estimate=pl.CostEstimate(
            flops=0, bytes_accessed=count * ROWS * columns * 4, transcendentals=0
        ),
        name="arrange",
    )(place, *parts, *after)


def finish_kernel(*refs):
    total = refs[0][...].astype(F32)
    for part in refs[1:-1]:
        total += part[...].astype(F32)
    refs[-1][...] = total


def finish(parts):
    return pl.pallas_call(
        finish_kernel,
        out_shape=jax.ShapeDtypeStruct(parts[0].shape, F32),
        in_specs=[VMEM] * len(parts),
        out_specs=VMEM,
        compiler_params=pltpu.CompilerParams(vmem_limit_bytes=8 << 20),
        name="finish",
    )(*parts)


def spread_over_layers(ready):
    ready = ready.reshape(NL * NX, 4 * ROWS, ready.shape[-1])
    passing = to_layer(ready[0:2], 0, 1)
    parts = [ready[4], to_layer(ready[5], 1, 0)]
    parts += [to_layer(ready[2], 0, 3), to_layer(ready[3], 1, 3)]
    joint = (ready[6:8].astype(F32) + passing.astype(F32)).astype(BF16)
    return parts + [to_layer(joint[0], 0, 1), to_layer(joint[1], 1, 1)]


def halves_kernel(behind_ref, ahead_ref, *refs):
    first_ref, second_ref = refs[-2:]
    rows = first_ref.shape[0]
    first_ref[...] = behind_ref[:rows, :]
    second_ref[...] = ahead_ref[rows:, :]


def halves(behind, ahead, after):
    rows, columns = behind.shape
    return pl.pallas_call(
        halves_kernel,
        out_shape=(jax.ShapeDtypeStruct((rows // 2, columns), behind.dtype),) * 2,
        in_specs=[VMEM, VMEM] + [ANY] * len(after),
        out_specs=(VMEM, VMEM),
        compiler_params=pltpu.CompilerParams(vmem_limit_bytes=4 << 20),
        name="halves",
    )(behind, ahead, *after)


def both_ways(own, axis):
    return send(own, **{axis: 1}), send(own, **{axis: -1})


def body(query_grads, doc_grads, out_basis, in_basis, eigenvalues, damping):
    place = jnp.stack([lax.axis_index("example"), lax.axis_index("layer")])

    own, docs = query_grads[0], doc_grads[0]
    docs_there = send(docs, dc=1)

    near = both_ways(own, "dz")
    row = pack(in_basis[0], eigenvalues[0], out_basis[0])
    pair = join([row, send(row, dc=1)], [])
    column = [send(pair, dy=d) for d in range(1, NY)]
    plane = join([pair] + column, [])
    pieces = [plane] + [send(plane, dz=d) for d in range(1, NZ)]
    tables = prepare(place, damping, pieces, [])

    cut = halves(*near, pieces[1:3])
    far = send(cut[0], dz=1), send(cut[1], dz=-1)

    side = rotate(tables, (own, *near), [cut[0]])
    side_y = both_ways(side, "dy")
    other = rotate(tables, far, [side], 20_000_000_000)
    other_y = both_ways(other, "dy")

    docs_other = held(docs_there, [other])

    def scored(blocks, after):
        conditioned = join(blocks, after)
        theirs = send(scores_of(conditioned, docs_other), dc=1)
        return [scores_of(conditioned, docs), theirs]

    parts = scored((side, other), [docs_other])

    low = join([side_y[1]], parts[:1], [(ROWS, 3 * ROWS)])
    high = join([side_y[0], other_y[0]], parts[:1], [(0, ROWS), (0, ROWS)])
    side_far = send(high, dy=1), send(low, dy=-1)
    parts += scored((*side_y, *other_y), [high, low])
    parts += scored(side_far, parts[2:3])

    offsets = [
        [(0, 0), (0, 1), (0, -1), (0, 2)],
        [(1, 0), (1, 1), (1, -1), (-1, 0), (-1, 1), (-1, -1), (1, 2), (-1, 2)],
        [(2, 0), (2, 2), (2, 1), (2, -1)],
    ]
    return finish(spread_over_layers(arrange(place, offsets, parts, [])))


def solution(mesh):
    placed = P("layer", "example", None)
    return jax.shard_map(
        body,
        mesh=mesh,
        in_specs=(placed,) * 5 + (P("layer"),),
        out_specs=P("layer", "example"),
        check_vma=False,
    )
```
